256 devices in a mesh: band: 32 (over y_lo, z, core), fft: 8 (over y_hi, x).
Axes of the slice: x: 4, y: 4 (y_hi: 2, y_lo: 2; y = y_hi * 2 + y_lo), z: 8, core: 2. Of those that a mesh axis runs over, the one named last changes fastest.
Arguments:
- orbitals: float32 [32, 2, 96, 9216], P('band', None, 'fft'), may hold values from -3 to 3
- serve_order: int32 [32], replicated, may hold values from 0 to 31, each once
Outputs:
- applied: float32 [32, 2, 96, 9216], P('band', None, 'fft')
- serving_exchange: float32 [2, 2, 96, 9216], P(None, None, 'fft', 'band')
The draws below stay inside these ranges and needn't reach their ends.
Inputs may be any that keep to these rules, and one draw needn't show every extreme that they name: `serve_order`: a permutation of the 32 band numbers.
All inputs are finite; a program needn't handle non-finite values.
Results may differ from the reference program's by a relative error of at most 0.0001.
Values sent between devices are 32-bit elements; how exact they have to be, the bound alone decides.
No kernel may reach another device: no remote copies, remote signals or barrier semaphores. Data moves between devices by JAX's collectives and lax.ppermute only.
A program may use at most 320 MiB of HBM per device.

```python
import math
import jax
import jax.numpy as jnp
from jax import lax

NX = 96
NY = 96
NZ = 96
SERVE = 2
NB = 32


def draw_orbitals(key, part):
    first = jax.random.fold_in(key, 0)
    shape = (NB, 2, NX, NY * NZ)
    return jnp.clip(0.5 * jax.random.normal(first, shape, dtype=jnp.float32), -3.0, 3.0)


def setup_inputs(seed: int = 0) -> dict:
    arg_keys = jax.random.split(jax.random.key(seed), 3)
    return {
        "orbitals": draw_orbitals(jax.random.fold_in(arg_keys[2], 71), 0),
        "serve_order": jax.random.permutation(arg_keys[1], NB).astype(jnp.int32),
    }


cell_side = 41.04
mixing = 0.25

def frequencies(count):
    signed = (jnp.arange(count, dtype=jnp.int32) + count // 2) % count - count // 2
    return signed.astype(jnp.float32) * (2.0 * math.pi / cell_side)

def coulomb_kernel():
    freq_x = frequencies(NX)
    freq_y = frequencies(NY)
    freq_z = frequencies(NZ)
    squared = freq_x[:, None, None] ** 2 + freq_y[None, :, None] ** 2 + freq_z[None, None, :] ** 2
    radius = cell_side * (3.0 / (4.0 * math.pi)) ** (1.0 / 3.0)
    safe_square = jnp.where(squared > 0, squared, 1.0)
    general = 4.0 * math.pi * (1.0 - jnp.cos(jnp.sqrt(safe_square) * radius)) / safe_square
    return jnp.where(squared > 0, general, 2.0 * math.pi * radius * radius)

def reference(orbitals, serve_order):
    kernel = coulomb_kernel()
    fields = (orbitals[:, 0] + 1j * orbitals[:, 1]).reshape(NB, NX, NY, NZ)
    served = fields[serve_order[:SERVE]]

    def per_band(running, orbital):
        density = jnp.conj(served) * orbital[None]
        potential = jnp.fft.ifftn(kernel[None] * jnp.fft.fftn(density, axes=(1, 2, 3)), axes=(1, 2, 3))
        result = -mixing * lax.optimization_barrier(jnp.sum(served * potential, axis=0))
        running = running + orbital[None] * jnp.conj(potential)
        return (running, result)
    totals, results = lax.scan(per_band, jnp.zeros_like(served), fields)
    totals = -mixing * totals
    applied = jnp.stack([jnp.real(results), jnp.imag(results)], axis=1).reshape(NB, 2, NX, NY * NZ).astype(jnp.float32)
    serving_exchange = jnp.stack([jnp.real(totals), jnp.imag(totals)], axis=1).reshape(SERVE, 2, NX, NY * NZ).astype(jnp.float32)
    return (applied, serving_exchange)
```

```python
import math

import jax
import jax.numpy as jnp
from jax import lax
from jax.sharding import PartitionSpec as P

NX = 96
NY = 96
NZ = 96
SERVE = 2
CHIPS = 16
ROWS = 24
PLANE = NY * NZ

cell_side = 41.04
mixing = 0.25


def frequencies(count):
    signed = (jnp.arange(count, dtype=jnp.int32) + count // 2) % count - count // 2
    return signed.astype(jnp.float32) * (2.0 * math.pi / cell_side)


def kernel_columns(start, width):
    freq_x = frequencies(NX)
    freq_y = lax.dynamic_slice_in_dim(frequencies(NY), start, width)
    freq_z = frequencies(NZ)
    squared = freq_x[:, None, None] ** 2 + freq_y[None, :, None] ** 2 + freq_z[None, None, :] ** 2
    radius = cell_side * (3.0 / (4.0 * math.pi)) ** (1.0 / 3.0)
    safe_square = jnp.where(squared > 0, squared, 1.0)
    general = 4.0 * math.pi * (1.0 - jnp.cos(jnp.sqrt(safe_square) * radius)) / safe_square
    return jnp.where(squared > 0, general, 2.0 * math.pi * radius * radius)


def dft_tables(count):
    indices = jnp.arange(count, dtype=jnp.int32)
    product = indices[:, None] * indices[None, :] % count
    angles = product.astype(jnp.float32) * (2.0 * math.pi / count)
    cosine = jnp.cos(angles)
    sine = jnp.sin(angles)
    forward = jnp.stack(
        [jnp.stack([cosine, sine], axis=1), jnp.stack([-sine, cosine], axis=1)], axis=0
    )
    inverse = jnp.stack(
        [jnp.stack([cosine, -sine], axis=1), jnp.stack([sine, cosine], axis=1)], axis=0
    )
    return (forward, inverse)


def transform(field, einsum_form, table):
    return jnp.einsum(einsum_form, table, field, precision=lax.Precision.HIGHEST)


def conj_times(left, right):
    lr, li = left[:12], left[12:]
    rr, ri = right[:12], right[12:]
    return jnp.concatenate([lr * rr + li * ri, lr * ri - li * rr], axis=0)


def times(left, right):
    lr, li = left[:12], left[12:]
    rr, ri = right[:12], right[12:]
    return jnp.concatenate([lr * rr - li * ri, lr * ri + li * rr], axis=0)


def shards(orbitals, serve_order):
    rank_fft = lax.axis_index("fft")
    rank_band = lax.axis_index("band")
    core = rank_band % 2
    chip = rank_band // 2
    swap = [(i, i ^ 1) for i in range(32)]
    same_core = [[2 * i + c for i in range(CHIPS)] for c in range(2)]
    table = dft_tables(96)
    kernel = kernel_columns(rank_fft * 12, 12).reshape(NX, 12, NZ) * (1.0 / (NX * NY * NZ))

    def chips_exchange(blocks):
        return lax.all_to_all(blocks, "band", 0, 0, axis_index_groups=same_core, tiled=True)

    def fft_exchange(blocks):
        return lax.all_to_all(blocks, "fft", 0, 0, tiled=True)

    mine = orbitals.reshape(ROWS, PLANE)
    other = lax.ppermute(mine, "band", swap)
    serving = serve_order[core]
    candidate = jnp.where(serving % 2 == core, mine, other)
    blocks = candidate.reshape(ROWS, CHIPS, PLANE // CHIPS).transpose(1, 0, 2)
    blocks = chips_exchange(blocks)
    block = lax.dynamic_index_in_dim(blocks, serving // 2, 0, keepdims=True)
    blocks = chips_exchange(jnp.broadcast_to(block, blocks.shape))
    served = blocks.transpose(1, 0, 2).reshape(ROWS, PLANE)

    density = jnp.stack([conj_times(served, mine), conj_times(served, other)])
    field = density.reshape(2, 2, 12, NY, NZ)
    field = transform(field, "akbz,pbxyz->paxyk", table[0])
    field = transform(field, "akby,pbxyz->paxkz", table[0])
    blocks = field.reshape(2, ROWS, 8, 12 * NZ).transpose(2, 0, 1, 3)
    blocks = fft_exchange(blocks)
    field = blocks.reshape(8, 2, 2, 12, 12, NZ).transpose(1, 2, 0, 3, 4, 5).reshape(2, 2, NX, 12, NZ)
    field = transform(field, "akbx,pbxyz->pakyz", table[0])
    field = field * kernel
    field = transform(field, "akbx,pbxyz->pakyz", table[1])
    blocks = field.reshape(2, 2, 8, 12, 12 * NZ).transpose(2, 0, 1, 3, 4).reshape(8, 2, ROWS, 12 * NZ)
    blocks = fft_exchange(blocks)
    field = blocks.transpose(1, 2, 0, 3).reshape(2, 2, 12, NY, NZ)
    field = transform(field, "akby,pbxyz->paxkz", table[1])
    field = transform(field, "akbz,pbxyz->paxyk", table[1])
    potential = field.reshape(2, ROWS, PLANE)

    sent = lax.ppermute(times(served, potential[1]), "band", swap)
    applied = -mixing * (times(served, potential[0]) + sent)
    terms = conj_times(potential[0], mine) + conj_times(potential[1], other)
    blocks = terms.reshape(ROWS, CHIPS, PLANE // CHIPS).transpose(1, 0, 2)
    blocks = chips_exchange(blocks)
    summed = -mixing * jnp.sum(blocks, axis=0)
    half = PLANE // CHIPS // 2
    keep = lax.dynamic_slice_in_dim(summed, core * half, half, 1)
    give = lax.dynamic_slice_in_dim(summed, (1 - core) * half, half, 1)
    got = lax.ppermute(give, "band", swap)
    first = jnp.where(core == 0, keep, got)
    second = jnp.where(core == 0, got, keep)
    serving_exchange = jnp.stack([first, second]).reshape(SERVE, 2, 12, half)
    return (applied.reshape(1, 2, 12, PLANE), serving_exchange)


def solution(mesh):
    return jax.shard_map(
        shards,
        mesh=mesh,
        in_specs=(P("band", None, "fft", None), P()),
        out_specs=(P("band", None, "fft", None), P(None, None, "fft", "band")),
        check_vma=False,
    )
```

```python
import functools
import math

import jax
import jax.numpy as jnp
import ml_dtypes
import numpy as np
from jax import lax
from jax.experimental import pallas as pl
from jax.experimental.pallas import tpu as pltpu
from jax.sharding import PartitionSpec as P

NX = 96
NY = 96
NZ = 96
SERVE = 2
CHIPS = 16
PARTS = 8
ROWS = 24
PLANE = NY * NZ
BLOCK = PLANE // PARTS
CHUNK = 112
HALF = PLANE // CHIPS // 2
VMEM = 48 * 1024 * 1024

cell_side = 41.04
mixing = 0.25


def frequencies(count):
    signed = (jnp.arange(count, dtype=jnp.int32) + count // 2) % count - count // 2
    return signed.astype(jnp.float32) * (2.0 * math.pi / cell_side)


def kernel_columns(start, width):
    freq_x = frequencies(NX)
    freq_y = lax.dynamic_slice_in_dim(frequencies(NY), start, width)
    freq_z = frequencies(NZ)
    freq_y = jnp.broadcast_to(freq_y[:, None], (width, NZ)).reshape(-1)
    freq_z = jnp.broadcast_to(freq_z[None], (width, NZ)).reshape(-1)
    squared = freq_x[:, None] ** 2 + freq_y[None] ** 2 + freq_z[None] ** 2
    radius = cell_side * (3.0 / (4.0 * math.pi)) ** (1.0 / 3.0)
    safe_square = jnp.where(squared > 0, squared, 1.0)
    general = 4.0 * math.pi * (1.0 - jnp.cos(jnp.sqrt(safe_square) * radius)) / safe_square
    return jnp.where(squared > 0, general, 2.0 * math.pi * radius * radius)


def split_table(table):
    high = table.astype(ml_dtypes.bfloat16)
    low = (table - high.astype(np.float64)).astype(ml_dtypes.bfloat16)
    return high, low


def angle_tables(sign):
    index = np.arange(96)
    angles = 2.0 * np.pi * (np.outer(index, index) % 96) / 96
    return np.cos(angles), sign * np.sin(angles)


def lane_table(sign):
    cosine, sine = angle_tables(sign)
    table = np.zeros((256, 256))
    table[:96, :96] = cosine
    table[128:224, 128:224] = cosine
    table[:96, 128:224] = sine
    table[128:224, :96] = -sine
    return split_table(table)


def slab_order():
    part = np.array([0] * 8 + [1] * 8 + [0] * 4 + [1] * 4)
    plane = np.array(list(range(8)) * 2 + list(range(8, 12)) * 2)
    part = np.tile(part, PARTS)
    plane = np.concatenate([plane + 12 * f for f in range(PARTS)])
    return part * 96 + plane


def row_tables():
    order = slab_order()
    cosine, sine = angle_tables(-1.0)
    forward = np.block([[cosine, -sine], [sine, cosine]])[:, order]
    cosine, sine = angle_tables(1.0)
    inverse = np.block([[cosine, -sine], [sine, cosine]])[order]
    return split_table(forward) + split_table(inverse)


def const_times(value, angle, count):
    re, im = value
    angle %= count
    if angle == 0:
        return value
    if 2 * angle == count:
        return (-re, -im)
    if 4 * angle == count:
        return (-im, re)
    if 4 * angle == 3 * count:
        return (im, -re)
    c = math.cos(2 * math.pi * angle / count)
    s = math.sin(2 * math.pi * angle / count)
    if (8 * angle) % count == 0:
        r = math.sqrt(0.5)
        c = math.copysign(1.0, c)
        s = math.copysign(1.0, s)
        a = re * (c * r)
        b = im * (c * r)
        return (a - b, a + b) if c == s else (a + b, b - a)
    return (re * c - im * s, re * s + im * c)


def add(a, b):
    return (a[0] + b[0], a[1] + b[1])


def sub(a, b):
    return (a[0] - b[0], a[1] - b[1])


def small_dft(x, sign):
    n = len(x)
    if n == 2:
        return [add(x[0], x[1]), sub(x[0], x[1])]
    if n == 3:
        total = add(x[1], x[2])
        diff = sub(x[1], x[2])
        r = sign * math.sqrt(0.75)
        mid = (x[0][0] - 0.5 * total[0], x[0][1] - 0.5 * total[1])
        turn = (-r * diff[1], r * diff[0])
        return [add(x[0], total), add(mid, turn), sub(mid, turn)]
    if n == 4:
        a, b = add(x[0], x[2]), sub(x[0], x[2])
        c, d = add(x[1], x[3]), sub(x[1], x[3])
        d = const_times(d, sign, 4)
        return [add(a, c), add(b, d), sub(a, c), sub(b, d)]
    inner = 4
    outer = n // inner
    out = [None] * n
    columns = []
    for low in range(outer):
        column = small_dft([x[outer * i + low] for i in range(inner)], sign)
        columns.append([const_times(v, sign * low * k, n) for k, v in enumerate(column)])
    for k in range(inner):
        row = small_dft([columns[low][k] for low in range(outer)], sign)
        for j in range(outer):
            out[k + inner * j] = row[j]
    return out


def leading_dft(field, sign):
    def tile(t, carry):
        rows = pl.ds(pl.multiple_of(t * 8, 8), 8)

        def load(y):
            return (field[y, rows, 0:128], field[y, rows, 128:256])

        def save(y, v):
            field[y, rows, 0:128] = v[0]
            field[y, rows, 128:256] = v[1]

        for low in range(8):
            column = small_dft([load(8 * i + low) for i in range(12)], sign)
            for k, v in enumerate(column):
                save(8 * k + low, const_times(v, sign * low * k, 96))
        return carry

    lax.fori_loop(0, 3, tile, 0)


def second_pass(field, k, rows, sign):
    values = [
        (field[8 * k + low, rows, 0:128], field[8 * k + low, rows, 128:256]) for low in range(8)
    ]
    return small_dft(values, sign)


def whole_dft(source, target, sign):
    leading_dft(source, sign)

    def tile(t, carry):
        rows = pl.ds(pl.multiple_of(t * 8, 8), 8)
        for k in range(12):
            for j, v in enumerate(second_pass(source, k, rows, sign)):
                target[k + 12 * j, rows, 0:128] = v[0]
                target[k + 12 * j, rows, 128:256] = v[1]
        return carry

    lax.fori_loop(0, 3, tile, 0)


def lanes():
    return lax.broadcasted_iota(jnp.int32, (8, 128), 1)


def unpack(wide):
    lane = lanes()
    out = []
    for q in range(3):
        a, b, c = (wide[:, 128 * (3 * q + i) : 128 * (3 * q + i + 1)] for i in range(3))
        out.append(a)
        out.append(jnp.where(lane < 32, pltpu.roll(a, 32, 1), pltpu.roll(b, 32, 1)))
        out.append(jnp.where(lane < 64, pltpu.roll(b, 64, 1), pltpu.roll(c, 64, 1)))
        out.append(pltpu.roll(c, 96, 1))
    return out


def pack(tiles):
    lane = lanes()
    out = []
    for q in range(3):
        a, b, c, d = tiles[4 * q : 4 * q + 4]
        b = pltpu.roll(b, 96, 1)
        c = pltpu.roll(c, 64, 1)
        d = pltpu.roll(d, 32, 1)
        out.append(jnp.where(lane < 96, a, b))
        out.append(jnp.where(lane < 64, b, c))
        out.append(jnp.where(lane < 32, c, d))
    return jnp.concatenate(out, axis=1)


def flip(x):
    return pltpu.roll(x, 4, 0)


def top(x):
    return lax.broadcasted_iota(jnp.int32, x.shape, 0) < 4


def split_dot(x, high, low):
    x_high = x.astype(jnp.bfloat16)
    x_low = (x - x_high.astype(jnp.float32)).astype(jnp.bfloat16)
    dot = functools.partial(jnp.dot, preferred_element_type=jnp.float32)
    return dot(x_high, high) + (dot(x_high, low) + dot(x_low, high))


def dot_split(high, low, x):
    x_high = x.astype(jnp.bfloat16)
    x_low = (x - x_high.astype(jnp.float32)).astype(jnp.bfloat16)
    dot = functools.partial(jnp.dot, preferred_element_type=jnp.float32)
    return dot(high, x_high) + (dot(low, x_high) + dot(high, x_low))


def tile_rows(ref, r, g):
    start = pl.multiple_of(8 * (72 * r + 9 * g), 8)
    x = ref[pl.ds(start, 72), :]
    return jnp.concatenate([x[8 * i : 8 * i + 8] for i in range(9)], axis=1)


def orbital_rows(ref, g):
    cols = pl.ds(pl.multiple_of(g * BLOCK, 128), BLOCK)
    rest = jnp.concatenate([ref[0, 8:12, cols], ref[1, 8:12, cols]], axis=0)
    return ref[0, 0:8, cols], ref[1, 0:8, cols], rest


def candidate_kernel(own_ref, mine, other, out):
    def copy(ref):
        for l in range(72):
            cols = slice(128 * l, 128 * l + 128)
            out[8 * l : 8 * l + 8, :] = ref[0, 0:8, cols]
            out[8 * (72 + l) : 8 * (72 + l) + 8, :] = ref[1, 0:8, cols]
            out[8 * (144 + l) : 8 * (144 + l) + 8, :] = jnp.concatenate(
                [ref[0, 8:12, cols], ref[1, 8:12, cols]], axis=0
            )

    out[1728:1792, :] = jnp.zeros((64, 128), jnp.float32)

    @pl.when(own_ref[0] == 1)
    def _():
        copy(mine)

    @pl.when(own_ref[0] == 0)
    def _():
        copy(other)


def forward_kernel(served, mine, other, high, low, out, line, field, spectrum):
    def block(g, carry):
        s0, s1, s2 = (tile_rows(served, r, g) for r in range(3))
        parts = []
        rests = []
        for ref in (mine, other):
            re, im, rest = orbital_rows(ref, g)
            parts.append((s0 * re + s1 * im, s0 * im - s1 * re))
            same = s2 * rest
            cross = s2 * flip(rest)
            rests.append((same + flip(same), cross - flip(cross)))
        upper = top(s2)
        parts.append(
            (jnp.where(upper, rests[0][0], rests[1][0]), jnp.where(upper, rests[0][1], -rests[1][1]))
        )
        for t, (re, im) in enumerate(parts):
            for y, (a, b) in enumerate(zip(unpack(re), unpack(im))):
                line[24 * y + 8 * t : 24 * y + 8 * t + 8, 0:128] = a
                line[24 * y + 8 * t : 24 * y + 8 * t + 8, 128:256] = b
        result = split_dot(line[...], high[...], low[...])
        field[pl.ds(g * 12, 12)] = result.reshape(12, 24, 256)
        return carry

    lax.fori_loop(0, PARTS, block, 0)
    whole_dft(field, spectrum, -1)

    def send(g, carry):
        packed = []
        for t in range(3):
            rows = slice(8 * t, 8 * t + 8)
            packed.append(
                tuple(
                    pack([spectrum[g * 12 + y, rows, c : c + 128] for y in range(12)])
                    for c in (0, 128)
                )
            )
        re, im = packed[2]
        upper = top(re)
        for p, rest in enumerate(
            (jnp.where(upper, re, flip(im)), jnp.where(upper, flip(re), im))
        ):
            out[g, p, 0:8, :] = packed[p][0]
            out[g, p, 8:16, :] = packed[p][1]
            out[g, p, 16:24, :] = rest
        return carry

    lax.fori_loop(0, PARTS, send, 0)


def column_kernel(blocks, coulomb, fh, fl, ih, il, out):
    x = blocks[:, 0].reshape(8 * ROWS, BLOCK)
    x = dot_split(fh[...], fl[...], x)
    k = coulomb[...]
    x = jnp.concatenate([x[:96] * k, x[96:] * k], axis=0)
    x = dot_split(ih[...], il[...], x)
    out[:, 0] = x.reshape(8, ROWS, BLOCK)


def backward_kernel(blocks, served, mine, other, high, low, own, away, terms, line, field, spectrum):
    def receive(g, carry):
        rests = [blocks[g, p, 16:24, :] for p in range(2)]
        upper = top(rests[0])
        parts = [(blocks[g, p, 0:8, :], blocks[g, p, 8:16, :]) for p in range(2)]
        parts.append(
            (
                jnp.where(upper, rests[0], flip(rests[1])),
                jnp.where(upper, flip(rests[0]), rests[1]),
            )
        )
        for t, (re, im) in enumerate(parts):
            rows = slice(8 * t, 8 * t + 8)
            for y, (a, b) in enumerate(zip(unpack(re), unpack(im))):
                spectrum[g * 12 + y, rows, 0:128] = a
                spectrum[g * 12 + y, rows, 128:256] = b
        return carry

    lax.fori_loop(0, PARTS, receive, 0)
    whole_dft(spectrum, field, 1)

    def block(g, carry):
        x = field[pl.ds(g * 12, 12)].reshape(288, 256)
        line[...] = split_dot(x, high[...], low[...])
        packed = []
        for t in range(3):
            packed.append(
                tuple(
                    pack([line[24 * y + 8 * t : 24 * y + 8 * t + 8, c : c + 128] for y in range(12)])
                    for c in (0, 128)
                )
            )
        re, im = packed[2]
        upper = top(re)
        rests = (jnp.where(upper, re, flip(im)), jnp.where(upper, flip(re), im))
        s0, s1, s2 = (tile_rows(served, r, g) for r in range(3))
        cols = pl.ds(pl.multiple_of(g * BLOCK, 128), BLOCK)
        sums = None
        for p, (ref, result) in enumerate(((mine, own), (other, away))):
            vr, vi = packed[p]
            v2 = rests[p]
            result[0, 0:8, cols] = s0 * vr - s1 * vi
            result[1, 0:8, cols] = s0 * vi + s1 * vr
            same = s2 * v2
            cross = s2 * flip(v2)
            result[0, 8:12, cols] = (same - flip(same))[0:4]
            result[1, 8:12, cols] = (cross + flip(cross))[0:4]
            ore, oim, rest = orbital_rows(ref, g)
            same = v2 * rest
            cross = v2 * flip(rest)
            turned = flip(cross)
            both = (
                vr * ore + vi * oim,
                vr * oim - vi * ore,
                jnp.where(upper, same + flip(same), turned - cross),
            )
            sums = both if sums is None else tuple(a + b for a, b in zip(sums, both))
        lane = lanes()
        for odd in range(2):
            start = pl.multiple_of((2 * g + odd) * CHUNK, 8)
            for r in range(3):
                for l in range(4):
                    c = 128 * (l + 5 * odd)
                    terms[pl.ds(start + 8 * (4 * r + l), 8), :] = sums[r][:, c : c + 128]
            h0, h1, h2 = (x[:, 512:640] for x in sums)
            if odd:
                h0, h2 = pltpu.roll(h0, 64, 1), pltpu.roll(h2, 64, 1)
            else:
                h1 = pltpu.roll(h1, 64, 1)
            terms[pl.ds(start + 96, 8), :] = jnp.where(lane < 64, h0, h1)
            terms[pl.ds(start + 104, 8), :] = h2
        return carry

    lax.fori_loop(0, PARTS, block, 0)


def finish_kernel(place, blocks, keep, give):
    lane = lanes()
    odd = place[1] == 1
    first_core = place[0] == 0
    tiles = []
    for i in range(14):
        x = [blocks[CHUNK * q + 8 * i : CHUNK * q + 8 * i + 8, :] for q in range(CHIPS)]
        while len(x) > 1:
            x = [x[2 * j] + x[2 * j + 1] for j in range(len(x) // 2)]
        tiles.append(x[0])
    halves = (tiles[12], pltpu.roll(tiles[12], 64, 1), tiles[13])
    for r in range(3):
        f = tiles[4 * r : 4 * r + 4]
        h = halves[r]
        s = [pltpu.roll(x, 64, 1) for x in f]
        wide = [
            jnp.where(odd, jnp.where(lane < 64, a, b), c)
            for a, b, c in zip([h] + s, s + [s[3]], f + [h])
        ]
        s = [pltpu.roll(x, 96, 1) for x in wide[2:]]
        second = [jnp.where(lane < 96, s[0], s[1]), jnp.where(lane < 96, s[1], s[2]), s[2]]
        first = wide[:3]
        for ref, cond in ((keep, first_core), (give, jnp.logical_not(first_core))):
            for i in range(3):
                x = jnp.where(cond, first[i], second[i])
                if i == 2:
                    x = x[:, :32]
                cols = slice(128 * i, 128 * i + x.shape[1])
                if r < 2:
                    ref[r, 0:8, cols] = x
                else:
                    ref[0, 8:12, cols] = x[0:4]
                    ref[1, 8:12, cols] = x[4:8]


def f32(*shape):
    return jax.ShapeDtypeStruct(shape, jnp.float32)


def shards(orbitals, serve_order):
    rank_fft = lax.axis_index("fft")
    rank_band = lax.axis_index("band")
    core = rank_band % 2
    chip = rank_band // 2
    swap = [(i, i ^ 1) for i in range(32)]
    same_core = [[2 * i + c for i in range(CHIPS)] for c in range(2)]
    scale = -mixing / (NX * NY * NZ)
    coulomb = kernel_columns(rank_fft * 12, 12) * scale
    params = pltpu.CompilerParams(vmem_limit_bytes=VMEM)
    scalars = pl.BlockSpec(memory_space=pltpu.SMEM)
    whole = pl.BlockSpec(memory_space=pltpu.VMEM)

    def chips_exchange(blocks):
        return lax.all_to_all(blocks, "band", 0, 0, axis_index_groups=same_core, tiled=True)

    def fft_exchange(blocks):
        return lax.all_to_all(blocks, "fft", 0, 0, tiled=True)

    mine = orbitals.reshape(2, 12, PLANE)
    other = lax.ppermute(mine, "band", swap)
    serving = serve_order[core]
    own = (serving % 2 == core).astype(jnp.int32).reshape(1)
    blocks = pl.pallas_call(
        candidate_kernel,
        out_shape=f32(CHIPS * CHUNK, 128),
        in_specs=[scalars, whole, whole],
        out_specs=whole,
        compiler_params=params,
        name="candidate",
    )(own, mine, other)
    blocks = chips_exchange(blocks.reshape(CHIPS, CHUNK, 128))
    block = lax.dynamic_index_in_dim(blocks, serving // 2, 0, keepdims=True)
    served = chips_exchange(jnp.broadcast_to(block, blocks.shape)).reshape(CHIPS * CHUNK, 128)

    scratch = [
        pltpu.VMEM((288, 256), jnp.float32),
        pltpu.VMEM((NY, ROWS, 256), jnp.float32),
        pltpu.VMEM((NY, ROWS, 256), jnp.float32),
    ]
    high, low = lane_table(-1.0)
    blocks = pl.pallas_call(
        forward_kernel,
        out_shape=f32(PARTS, 2, ROWS, BLOCK),
        in_specs=[whole] * 5,
        out_specs=whole,
        scratch_shapes=scratch,
        compiler_params=params,
        name="forward",
    )(served, mine, other, jnp.asarray(high), jnp.asarray(low))
    blocks = fft_exchange(blocks)
    tables = [jnp.asarray(t) for t in row_tables()]
    fixed = pl.BlockSpec((192, 192), lambda p: (0, 0))
    pair = pl.BlockSpec((PARTS, 1, ROWS, BLOCK), lambda p: (0, p, 0, 0))
    blocks = pl.pallas_call(
        column_kernel,
        out_shape=f32(PARTS, 2, ROWS, BLOCK),
        grid=(2,),
        in_specs=[pair, pl.BlockSpec((NX, BLOCK), lambda p: (0, 0))] + [fixed] * 4,
        out_specs=pair,
        compiler_params=params,
        name="columns",
    )(blocks, coulomb, *tables)
    blocks = fft_exchange(blocks)
    high, low = lane_table(1.0)
    own, away, terms = pl.pallas_call(
        backward_kernel,
        out_shape=(f32(2, 12, PLANE), f32(2, 12, PLANE), f32(CHIPS * CHUNK, 128)),
        in_specs=[whole] * 6,
        out_specs=(whole,) * 3,
        scratch_shapes=scratch,
        compiler_params=params,
        name="backward",
    )(blocks, served, mine, other, jnp.asarray(high), jnp.asarray(low))
    applied = own + lax.ppermute(away, "band", swap)
    blocks = chips_exchange(terms.reshape(CHIPS, CHUNK, 128)).reshape(CHIPS * CHUNK, 128)
    place = jnp.stack([core, chip % 2]).astype(jnp.int32)
    keep, give = pl.pallas_call(
        finish_kernel,
        out_shape=(f32(2, 12, HALF), f32(2, 12, HALF)),
        in_specs=[scalars, whole],
        out_specs=(whole, whole),
        compiler_params=params,
        name="finish",
    )(place, blocks)
    got = lax.ppermute(give, "band", swap)
    first = jnp.where(core == 0, keep, got)
    second = jnp.where(core == 0, got, keep)
    serving_exchange = jnp.stack([first, second])
    return (applied.reshape(1, 2, 12, PLANE), serving_exchange)


def solution(mesh):
    return jax.shard_map(
        shards,
        mesh=mesh,
        in_specs=(P("band", None, "fft", None), P()),
        out_specs=(P("band", None, "fft", None), P(None, None, "fft", "band")),
        check_vma=False,
    )
```

```python
import functools
import math

import jax
import jax.numpy as jnp
import ml_dtypes
import numpy as np
from jax import lax
from jax.experimental import pallas as pl
from jax.experimental.pallas import tpu as pltpu
from jax.sharding import PartitionSpec as P

NX = 96
NY = 96
NZ = 96
SERVE = 2
CHIPS = 16
PARTS = 8
ROWS = 24
PLANE = NY * NZ
BLOCK = PLANE // PARTS
CHUNK = 112
LIST = 8 * CHUNK
TILES = 108 * 8
HALF = PLANE // CHIPS // 2
UNROLL = True
VMEM = 48 * 1024 * 1024

cell_side = 41.04
mixing = 0.25


def frequencies(count):
    signed = (jnp.arange(count, dtype=jnp.int32) + count // 2) % count - count // 2
    return signed.astype(jnp.float32) * (2.0 * math.pi / cell_side)


def kernel_columns(start, width):
    freq_x = frequencies(NX)
    freq_y = lax.dynamic_slice_in_dim(frequencies(NY), start, width)
    freq_z = frequencies(NZ)
    freq_y = jnp.broadcast_to(freq_y[:, None], (width, NZ)).reshape(-1)
    freq_z = jnp.broadcast_to(freq_z[None], (width, NZ)).reshape(-1)
    squared = freq_x[:, None] ** 2 + freq_y[None] ** 2 + freq_z[None] ** 2
    radius = cell_side * (3.0 / (4.0 * math.pi)) ** (1.0 / 3.0)
    safe_square = jnp.where(squared > 0, squared, 1.0)
    general = 4.0 * math.pi * (1.0 - jnp.cos(jnp.sqrt(safe_square) * radius)) / safe_square
    return jnp.where(squared > 0, general, 2.0 * math.pi * radius * radius)


def split_table(table):
    high = table.astype(ml_dtypes.bfloat16)
    low = (table - high.astype(np.float64)).astype(ml_dtypes.bfloat16)
    return high, low


def angle_tables(sign):
    index = np.arange(96)
    angles = 2.0 * np.pi * (np.outer(index, index) % 96) / 96
    return np.cos(angles), sign * np.sin(angles)


def lane_table(sign):
    cosine, sine = angle_tables(sign)
    table = np.zeros((256, 256))
    table[:96, :96] = cosine
    table[128:224, 128:224] = cosine
    table[:96, 128:224] = sine
    table[128:224, :96] = -sine
    return split_table(table)


def slab_order():
    part = np.array([0] * 8 + [1] * 8 + [0] * 4 + [1] * 4)
    virtual = np.array(list(range(8)) * 2 + list(range(8, 12)) * 2)
    slot = np.array([0, 0, 0, 0, 1, 1, 1, 1, 0, 0, 1, 1])[virtual]
    local = np.array([0, 1, 2, 3, 0, 1, 2, 3, 4, 5, 4, 5])[virtual]
    planes = np.array([[0, 1, 2, 3, 8, 9], [4, 5, 6, 7, 10, 11]])
    places = [
        slot * 192 + part * 96 + 12 * f + planes[half][local] for half in range(2) for f in range(PARTS)
    ]
    return np.concatenate(places)


def row_tables():
    order = slab_order()
    cosine, sine = angle_tables(-1.0)
    single = np.block([[cosine, -sine], [sine, cosine]])
    forward = np.kron(np.eye(2), single)[:, order]
    cosine, sine = angle_tables(1.0)
    single = np.block([[cosine, -sine], [sine, cosine]])
    inverse = np.kron(np.eye(2), single)[order]
    return split_table(forward) + split_table(inverse)


def const_times(value, angle, count):
    re, im = value
    angle %= count
    if angle == 0:
        return value
    if 2 * angle == count:
        return (-re, -im)
    if 4 * angle == count:
        return (-im, re)
    if 4 * angle == 3 * count:
        return (im, -re)
    c = math.cos(2 * math.pi * angle / count)
    s = math.sin(2 * math.pi * angle / count)
    if (8 * angle) % count == 0:
        r = math.sqrt(0.5)
        c = math.copysign(1.0, c)
        s = math.copysign(1.0, s)
        a = re * (c * r)
        b = im * (c * r)
        return (a - b, a + b) if c == s else (a + b, b - a)
    return (re * c - im * s, re * s + im * c)


def add(a, b):
    return (a[0] + b[0], a[1] + b[1])


def sub(a, b):
    return (a[0] - b[0], a[1] - b[1])


def small_dft(x, sign):
    n = len(x)
    if n == 2:
        return [add(x[0], x[1]), sub(x[0], x[1])]
    if n == 3:
        total = add(x[1], x[2])
        diff = sub(x[1], x[2])
        r = sign * math.sqrt(0.75)
        mid = (x[0][0] - 0.5 * total[0], x[0][1] - 0.5 * total[1])
        turn = (-r * diff[1], r * diff[0])
        return [add(x[0], total), add(mid, turn), sub(mid, turn)]
    if n == 4:
        a, b = add(x[0], x[2]), sub(x[0], x[2])
        c, d = add(x[1], x[3]), sub(x[1], x[3])
        d = const_times(d, sign, 4)
        return [add(a, c), add(b, d), sub(a, c), sub(b, d)]
    inner = 4
    outer = n // inner
    out = [None] * n
    columns = []
    for low in range(outer):
        column = small_dft([x[outer * i + low] for i in range(inner)], sign)
        columns.append([const_times(v, sign * low * k, n) for k, v in enumerate(column)])
    for k in range(inner):
        row = small_dft([columns[low][k] for low in range(outer)], sign)
        for j in range(outer):
            out[k + inner * j] = row[j]
    return out


def leading_dft(field, sign):
    def tile(t, carry):
        rows = pl.ds(pl.multiple_of(t * 8, 8), 8)

        def load(y):
            return (field[y, rows, 0:128], field[y, rows, 128:256])

        def save(y, v):
            field[y, rows, 0:128] = v[0]
            field[y, rows, 128:256] = v[1]

        for low in range(8):
            column = small_dft([load(8 * i + low) for i in range(12)], sign)
            for k, v in enumerate(column):
                save(8 * k + low, const_times(v, sign * low * k, 96))
        return carry

    lax.fori_loop(0, 3, tile, 0, unroll=UNROLL)


def second_pass(field, k, rows, sign):
    values = [
        (field[8 * k + low, rows, 0:128], field[8 * k + low, rows, 128:256]) for low in range(8)
    ]
    return small_dft(values, sign)


def whole_dft(source, target, sign):
    leading_dft(source, sign)

    def tile(t, carry):
        rows = pl.ds(pl.multiple_of(t * 8, 8), 8)
        for k in range(12):
            for j, v in enumerate(second_pass(source, k, rows, sign)):
                target[k + 12 * j, rows, 0:128] = v[0]
                target[k + 12 * j, rows, 128:256] = v[1]
        return carry

    lax.fori_loop(0, 3, tile, 0, unroll=UNROLL)


def lanes():
    return lax.broadcasted_iota(jnp.int32, (8, 128), 1)


def unpack(wide):
    lane = lanes()
    out = []
    for q in range(3):
        a, b, c = (wide[:, 128 * (3 * q + i) : 128 * (3 * q + i + 1)] for i in range(3))
        out.append(a)
        out.append(jnp.where(lane < 32, pltpu.roll(a, 32, 1), pltpu.roll(b, 32, 1)))
        out.append(jnp.where(lane < 64, pltpu.roll(b, 64, 1), pltpu.roll(c, 64, 1)))
        out.append(pltpu.roll(c, 96, 1))
    return out


def pack(tiles):
    lane = lanes()
    out = []
    for q in range(3):
        a, b, c, d = tiles[4 * q : 4 * q + 4]
        b = pltpu.roll(b, 96, 1)
        c = pltpu.roll(c, 64, 1)
        d = pltpu.roll(d, 32, 1)
        out.append(jnp.where(lane < 96, a, b))
        out.append(jnp.where(lane < 64, b, c))
        out.append(jnp.where(lane < 32, c, d))
    return jnp.concatenate(out, axis=1)


def flip(x):
    return pltpu.roll(x, 4, 0)


def top(x):
    return lax.broadcasted_iota(jnp.int32, x.shape, 0) < 4


def split_dot(x, high, low):
    x_high = x.astype(jnp.bfloat16)
    x_low = (x - x_high.astype(jnp.float32)).astype(jnp.bfloat16)
    dot = functools.partial(jnp.dot, preferred_element_type=jnp.float32)
    return dot(x_high, high) + (dot(x_high, low) + dot(x_low, high))


def dot_split(high, low, x):
    x_high = x.astype(jnp.bfloat16)
    x_low = (x - x_high.astype(jnp.float32)).astype(jnp.bfloat16)
    dot = functools.partial(jnp.dot, preferred_element_type=jnp.float32)
    return dot(high, x_high) + (dot(low, x_high) + dot(high, x_low))


def row_index(x):
    return lax.broadcasted_iota(jnp.int32, x.shape, 0)


def combine(a0, a1, b0, b1):
    upper = top(a0)
    row = row_index(b0)
    rest = jnp.where(
        row < 2,
        b0,
        jnp.where(
            row < 4,
            pltpu.roll(b1, 2, 0),
            jnp.where(row < 6, pltpu.roll(b0, 2, 0), pltpu.roll(b1, 4, 0)),
        ),
    )
    return jnp.where(upper, a0, flip(a1)), jnp.where(upper, flip(a0), a1), rest


def split(t0, t1, t2):
    upper = top(t0)
    low = row_index(t2) < 2
    back = pltpu.roll(t2, 6, 0)
    return (
        jnp.where(upper, t0, flip(t1)),
        jnp.where(upper, flip(t0), t1),
        jnp.where(low, t2, back),
        jnp.where(low, back, flip(t2)),
    )


def list_load(ref, start):
    x = ref[pl.ds(pl.multiple_of(start, 8), 72), :]
    return jnp.concatenate([x[8 * i : 8 * i + 8] for i in range(9)], axis=1)


def list_save(ref, start, x):
    for i in range(9):
        ref[pl.ds(pl.multiple_of(start + 8 * i, 8), 8), :] = x[:, 128 * i : 128 * i + 128]


def second_start(g):
    return 8 * (72 + 9 * lax.rem(g, 4))


def half_load(ref, g):
    b = list_load(ref, second_start(g))
    return list_load(ref, 72 * g), jnp.where(g >= 4, flip(b), b)


def half_save(ref, g, a, b):
    list_save(ref, 72 * g, a)
    old = list_load(ref, second_start(g))
    upper = top(b)
    b = jnp.where(upper, b, flip(b))
    b = jnp.where(g < 4, jnp.where(upper, b, old), jnp.where(upper, old, b))
    list_save(ref, second_start(g), b)


def block_columns(g):
    return pl.ds(pl.multiple_of(g * BLOCK, 128), BLOCK)


def slab_rows(ref, g):
    cols = block_columns(g)
    rest = jnp.concatenate([ref[0, 8:12, cols], ref[1, 8:12, cols]], axis=0)
    return ref[0, 0:8, cols], ref[1, 0:8, cols], rest


def orbital_rows(ref, g):
    cols = block_columns(g)
    return ref[0:8, cols], ref[8:16, cols], ref[16:24, cols]


def halves_kernel(place, orbital, keep, send):
    first = place[2] == 0

    def block(g, carry):
        a0, a1, b0, b1 = split(*slab_rows(orbital, g))
        half_save(keep, g, jnp.where(first, a0, a1), jnp.where(first, b0, b1))
        half_save(send, g, jnp.where(first, a1, a0), jnp.where(first, b1, b0))
        return carry

    lax.fori_loop(0, PARTS, block, 0, unroll=UNROLL)
    for ref in (keep, send):
        ref[TILES:LIST, :] = jnp.zeros((LIST - TILES, 128), jnp.float32)


def assemble_kernel(place, keep, recv, keep_other, recv_other, mine, other):
    first = place[2] == 0

    def block(g, carry):
        cols = block_columns(g)
        for own, far, out in ((keep, recv, mine), (keep_other, recv_other, other)):
            (a0, b0), (a1, b1) = half_load(own, g), half_load(far, g)
            rows = combine(
                jnp.where(first, a0, a1),
                jnp.where(first, a1, a0),
                jnp.where(first, b0, b1),
                jnp.where(first, b1, b0),
            )
            for r in range(3):
                out[8 * r : 8 * r + 8, cols] = rows[r]
        return carry

    lax.fori_loop(0, PARTS, block, 0, unroll=UNROLL)


def applied_kernel(place, near, got, far, out):
    first = place[2] == 0

    def block(g, carry):
        cols = block_columns(g)
        a0, b0 = half_load(near, g)
        a1, b1 = half_load(got, g)
        a0, b0 = a0 + a1, b0 + b1
        a1, b1 = half_load(far, g)
        t0, t1, t2 = combine(
            jnp.where(first, a0, a1),
            jnp.where(first, a1, a0),
            jnp.where(first, b0, b1),
            jnp.where(first, b1, b0),
        )
        out[0, 0:8, cols] = t0
        out[1, 0:8, cols] = t1
        out[0, 8:12, cols] = t2[0:4]
        out[1, 8:12, cols] = t2[4:8]
        return carry

    lax.fori_loop(0, PARTS, block, 0, unroll=UNROLL)


def served_rows(ref, g):
    a, b = half_load(ref, g)
    return combine(a, a, b, b)


def forward_kernel(place, served, mine, other, table, out, line, field, spectrum):
    def block(g, carry):
        s0, s1, s2 = served_rows(served, g)
        parts = []
        rests = []
        for ref in (mine, other):
            re, im, rest = orbital_rows(ref, g)
            parts.append((s0 * re + s1 * im, s0 * im - s1 * re))
            same = s2 * rest
            cross = s2 * flip(rest)
            rests.append((same + flip(same), cross - flip(cross)))
        upper = top(s2)
        parts.append(
            (jnp.where(upper, rests[0][0], rests[1][0]), jnp.where(upper, rests[0][1], -rests[1][1]))
        )
        for t, (re, im) in enumerate(parts):
            for y, (a, b) in enumerate(zip(unpack(re), unpack(im))):
                line[24 * y + 8 * t : 24 * y + 8 * t + 8, 0:128] = a
                line[24 * y + 8 * t : 24 * y + 8 * t + 8, 128:256] = b
        result = split_dot(line[...], table[0:256], table[256:512])
        field[pl.ds(g * 12, 12)] = result.reshape(12, 24, 256)
        return carry

    lax.fori_loop(0, PARTS, block, 0, unroll=UNROLL)
    whole_dft(field, spectrum, -1)

    def send(g, carry):
        packed = []
        for t in range(3):
            rows = slice(8 * t, 8 * t + 8)
            packed.append(
                tuple(
                    pack([spectrum[g * 12 + y, rows, c : c + 128] for y in range(12)])
                    for c in (0, 128)
                )
            )
        re, im = packed[2]
        upper = top(re)
        for p, rest in enumerate(
            (jnp.where(upper, re, flip(im)), jnp.where(upper, flip(re), im))
        ):
            out[p, g, 0:8, :] = packed[p][0]
            out[p, g, 8:16, :] = packed[p][1]
            out[p, g, 16:24, :] = rest
        return carry

    lax.fori_loop(0, PARTS, send, 0, unroll=UNROLL)


def column_kernel(blocks, coulomb, tables, out):
    lanes_here = blocks.shape[-1]
    x = blocks[...].reshape(16 * ROWS, lanes_here)
    x = dot_split(tables[0:384], tables[384:768], x)
    k = coulomb[...]
    x = jnp.concatenate([x[96 * i : 96 * i + 96] * k for i in range(4)], axis=0)
    x = dot_split(tables[768:1152], tables[1152:1536], x)
    out[...] = x.reshape(16, ROWS, lanes_here)


def backward_kernel(
    place, blocks, served, mine, other, table, own_near, own_far, away_near, away_far, terms,
    line, field, spectrum, total,
):
    first = place[2] == 0

    def receive(g, carry):
        rests = [blocks[p, g, 16:24, :] for p in range(2)]
        upper = top(rests[0])
        parts = [(blocks[p, g, 0:8, :], blocks[p, g, 8:16, :]) for p in range(2)]
        parts.append(
            (
                jnp.where(upper, rests[0], flip(rests[1])),
                jnp.where(upper, flip(rests[0]), rests[1]),
            )
        )
        for t, (re, im) in enumerate(parts):
            rows = slice(8 * t, 8 * t + 8)
            for y, (a, b) in enumerate(zip(unpack(re), unpack(im))):
                spectrum[g * 12 + y, rows, 0:128] = a
                spectrum[g * 12 + y, rows, 128:256] = b
        return carry

    lax.fori_loop(0, PARTS, receive, 0, unroll=UNROLL)
    whole_dft(spectrum, field, 1)

    def block(g, carry):
        x = field[pl.ds(g * 12, 12)].reshape(288, 256)
        line[...] = split_dot(x, table[0:256], table[256:512])
        packed = []
        for t in range(3):
            packed.append(
                tuple(
                    pack([line[24 * y + 8 * t : 24 * y + 8 * t + 8, c : c + 128] for y in range(12)])
                    for c in (0, 128)
                )
            )
        re, im = packed[2]
        upper = top(re)
        rests = (jnp.where(upper, re, flip(im)), jnp.where(upper, flip(re), im))
        s0, s1, s2 = served_rows(served, g)
        sums = None
        for p, (ref, near, far) in enumerate(
            ((mine, own_near, own_far), (other, away_near, away_far))
        ):
            vr, vi = packed[p]
            v2 = rests[p]
            same = s2 * v2
            cross = s2 * flip(v2)
            a0, a1, b0, b1 = split(
                s0 * vr - s1 * vi,
                s0 * vi + s1 * vr,
                jnp.where(upper, same - flip(same), cross + flip(cross)),
            )
            half_save(near, g, jnp.where(first, a0, a1), jnp.where(first, b0, b1))
            half_save(far, g, jnp.where(first, a1, a0), jnp.where(first, b1, b0))
            ore, oim, rest = orbital_rows(ref, g)
            same = v2 * rest
            cross = v2 * flip(rest)
            turned = flip(cross)
            both = (
                vr * ore + vi * oim,
                vr * oim - vi * ore,
                jnp.where(upper, same + flip(same), turned - cross),
            )
            sums = both if sums is None else tuple(a + b for a, b in zip(sums, both))
        a0, a1, b0, b1 = split(*sums)
        half_save(total, g, a0 + a1, b0 + b1)
        return carry

    lax.fori_loop(0, PARTS, block, 0, unroll=UNROLL)
    lane = lanes()

    def tile(l):
        return total[8 * l : 8 * l + 8, :]

    def turn(x):
        return pltpu.roll(x, 64, 1)

    for g in range(4):
        middle = 9 * g + 4
        for odd in range(2):
            begin = 9 * g + 5 * odd
            tiles = [tile(begin + i) for i in range(4)] + [tile(begin + 36 + i) for i in range(4)]
            a, b = tile(middle), tile(middle + 36)
            a, b = (turn(a), b) if odd else (a, turn(b))
            tiles.append(jnp.where(lane < 64, a, b))
            tiles += [tile(72 + begin + i) for i in range(4)]
            a = tile(72 + middle)
            tiles.append(turn(a) if odd else a)
            for i, x in enumerate(tiles):
                start = (2 * g + odd) * CHUNK + 8 * i
                terms[start : start + 8, :] = x


def finish_kernel(place, blocks, *pieces):
    lane = lanes()
    second_core = place[0] == 1
    odd = place[1] == 1
    second_half = place[2] == 1
    tiles = []
    for i in range(14):
        x = [blocks[CHUNK * q + 8 * i : CHUNK * q + 8 * i + 8, :] for q in range(8)]
        while len(x) > 1:
            x = [x[2 * j] + x[2 * j + 1] for j in range(len(x) // 2)]
        tiles.append(x[0])

    def widen(f, h):
        s = [pltpu.roll(x, 64, 1) for x in f]
        wide = [
            jnp.where(odd, jnp.where(lane < 64, a, b), c)
            for a, b, c in zip([h] + s, s + [s[3]], f + [h])
        ]
        s = [pltpu.roll(x, 96, 1) for x in wide[2:]]
        second = [jnp.where(lane < 96, s[0], s[1]), jnp.where(lane < 96, s[1], s[2]), s[2]]
        return wide[:3], second

    left = widen(tiles[0:4], tiles[8])
    right = widen(tiles[4:8], pltpu.roll(tiles[8], 64, 1))
    rest = widen(tiles[9:13], tiles[13])
    for piece, out in enumerate(pieces):
        half = second_half if piece < 2 else jnp.logical_not(second_half)
        core = second_core if piece % 2 == 0 else jnp.logical_not(second_core)
        for i in range(3):
            x = [jnp.where(core, y[1][i], y[0][i]) for y in (left, right, rest)]
            a = jnp.where(half, x[1], x[0])
            b = jnp.where(half, flip(x[2]), x[2])
            width = 128 if i < 2 else 32
            cols = slice(128 * i, 128 * i + width)
            out[0:8, cols] = a[:, :width]
            out[8:12, cols] = b[0:4, :width]


def serving_kernel(place, p00, p01, p10, p11, out):
    second_core = place[0] == 1
    second_half = place[2] == 1
    x = [[p00[...], p01[...]], [p10[...], p11[...]]]
    for member in range(2):
        swap = second_core if member == 0 else jnp.logical_not(second_core)
        near, far = (jnp.where(swap, x[i][1], x[i][0]) for i in range(2))
        h0 = jnp.where(second_half, far, near)
        h1 = jnp.where(second_half, near, far)
        for part in range(2):
            out[member, part, 0:4, :] = h0[4 * part : 4 * part + 4]
            out[member, part, 4:8, :] = h1[4 * part : 4 * part + 4]
            out[member, part, 8:10, :] = h0[8 + 2 * part : 10 + 2 * part]
            out[member, part, 10:12, :] = h1[8 + 2 * part : 10 + 2 * part]


def f32(*shape):
    return jax.ShapeDtypeStruct(shape, jnp.float32)


def shards(orbitals, serve_order):
    rank_fft = lax.axis_index("fft")
    rank_band = lax.axis_index("band")
    core = rank_band % 2
    line = rank_band // 2 % 8
    half = rank_band // 16
    place = jnp.stack([core, line % 2, half]).astype(jnp.int32)
    z_groups = [[y * 16 + 2 * z + c for z in range(8)] for y in range(2) for c in range(2)]
    plane_groups = [
        [(y * 16 + b) * PARTS + f for y in range(2) for f in range(PARTS)] for b in range(16)
    ]
    scale = -mixing / (NX * NY * NZ)

    coulomb = kernel_columns(rank_fft * 12, 12) * scale
    params = pltpu.CompilerParams(vmem_limit_bytes=VMEM)
    scalars = pl.BlockSpec(memory_space=pltpu.SMEM)
    whole = pl.BlockSpec(memory_space=pltpu.VMEM)

    def call(kernel, shapes, inputs, scratch=()):
        return pl.pallas_call(
            kernel,
            out_shape=shapes,
            in_specs=[scalars] + [whole] * len(inputs),
            out_specs=jax.tree.map(lambda _: whole, shapes),
            scratch_shapes=list(scratch),
            compiler_params=params,
        )(place, *inputs)

    def swap(x, bits):
        return lax.ppermute(x, "band", [(i, i ^ bits) for i in range(32)])

    def line_exchange(blocks):
        return lax.all_to_all(blocks, "band", 0, 0, axis_index_groups=z_groups, tiled=True)

    def plane_exchange(blocks):
        return lax.all_to_all(
            blocks, ("band", "fft"), 0, 0, axis_index_groups=plane_groups, tiled=True
        )

    lists = f32(LIST, 128)
    keep, send = call(halves_kernel, (lists, lists), (orbitals.reshape(2, 12, PLANE),))
    recv = swap(send, 16)
    keep_other = swap(keep, 1)
    recv_other = swap(recv, 1)
    serving = serve_order[core]
    near = serving // 16 == half
    same = serving % 2 == core
    candidate = jnp.where(
        same, jnp.where(near, keep, recv), jnp.where(near, keep_other, recv_other)
    )
    blocks = line_exchange(candidate.reshape(8, CHUNK, 128))
    block = lax.dynamic_index_in_dim(blocks, serving // 2 % 8, 0, keepdims=True)
    block, coulomb = lax.optimization_barrier((block, coulomb))
    served = line_exchange(jnp.broadcast_to(block, blocks.shape)).reshape(LIST, 128)
    rows = f32(ROWS, PLANE)
    mine, other = call(assemble_kernel, (rows, rows), (keep, recv, keep_other, recv_other))

    scratch = [
        pltpu.VMEM((288, 256), jnp.float32),
        pltpu.VMEM((NY, ROWS, 256), jnp.float32),
        pltpu.VMEM((NY, ROWS, 256), jnp.float32),
    ]
    table = jnp.asarray(np.concatenate(lane_table(-1.0)))
    blocks = call(
        forward_kernel, f32(2, PARTS, ROWS, BLOCK), (served, mine, other, table), scratch
    )
    blocks = plane_exchange(blocks.reshape(16, ROWS, BLOCK))
    tables = jnp.asarray(np.concatenate(row_tables()))
    fixed = pl.BlockSpec((4 * 384, 384), lambda i: (0, 0))
    piece = pl.BlockSpec((16, ROWS, BLOCK // 3), lambda i: (0, 0, i))
    blocks = pl.pallas_call(
        column_kernel,
        out_shape=f32(16, ROWS, BLOCK),
        grid=(3,),
        in_specs=[piece, pl.BlockSpec((NX, BLOCK // 3), lambda i: (0, i)), fixed],
        out_specs=piece,
        compiler_params=params,
    )(blocks, coulomb, tables)
    blocks = plane_exchange(blocks).reshape(2, PARTS, ROWS, BLOCK)
    table = jnp.asarray(np.concatenate(lane_table(1.0)))
    short = f32(TILES, 128)
    own_near, own_far, away_near, away_far, terms = call(
        backward_kernel,
        (short, short, short, short, lists),
        (blocks, served, mine, other, table),
        scratch + [pltpu.VMEM((TILES, 128), jnp.float32)],
    )
    far = swap(own_far + swap(away_far, 1), 16)
    got = swap(away_near, 1)
    applied = call(applied_kernel, f32(2, 12, PLANE), (own_near, got, far))
    blocks = line_exchange(terms.reshape(8, CHUNK, 128)).reshape(LIST, 128)
    blocks, applied = lax.optimization_barrier((blocks, applied))
    small = f32(12, HALF)
    pieces = call(finish_kernel, (small,) * 4, (blocks,))
    pieces = [pieces[0], swap(pieces[1], 1), swap(pieces[2], 16), swap(pieces[3], 17)]
    serving_exchange = call(serving_kernel, f32(SERVE, 2, 12, HALF), pieces)
    return (applied.reshape(1, 2, 12, PLANE), serving_exchange)


def solution(mesh):
    return jax.shard_map(
        shards,
        mesh=mesh,
        in_specs=(P("band", None, "fft", None), P()),
        out_specs=(P("band", None, "fft", None), P(None, None, "fft", "band")),
        check_vma=False,
    )
```

```python
import functools
import math

import jax
import jax.numpy as jnp
import ml_dtypes
import numpy as np
from jax import lax
from jax.experimental import pallas as pl
from jax.experimental.pallas import tpu as pltpu
from jax.sharding import PartitionSpec as P

NX = 96
NY = 96
NZ = 96
SERVE = 2
CHIPS = 16
PARTS = 8
ROWS = 24
PLANE = NY * NZ
BLOCK = PLANE // PARTS
CHUNK = 112
LIST = 8 * CHUNK
TILES = 108 * 8
HALF = PLANE // CHIPS // 2
UNROLL = True
VMEM = 48 * 1024 * 1024

cell_side = 41.04
mixing = 0.25


def frequencies(count):
    signed = (jnp.arange(count, dtype=jnp.int32) + count // 2) % count - count // 2
    return signed.astype(jnp.float32) * (2.0 * math.pi / cell_side)


def kernel_columns(start, width):
    freq_x = frequencies(NX)
    freq_y = lax.dynamic_slice_in_dim(frequencies(NY), start, width)
    freq_z = frequencies(NZ)
    freq_y = jnp.broadcast_to(freq_y[:, None], (width, NZ)).reshape(-1)
    freq_z = jnp.broadcast_to(freq_z[None], (width, NZ)).reshape(-1)
    squared = freq_x[:, None] ** 2 + freq_y[None] ** 2 + freq_z[None] ** 2
    radius = cell_side * (3.0 / (4.0 * math.pi)) ** (1.0 / 3.0)
    safe_square = jnp.where(squared > 0, squared, 1.0)
    general = 4.0 * math.pi * (1.0 - jnp.cos(jnp.sqrt(safe_square) * radius)) / safe_square
    return jnp.where(squared > 0, general, 2.0 * math.pi * radius * radius)


def split_table(table):
    high = table.astype(ml_dtypes.bfloat16)
    low = (table - high.astype(np.float64)).astype(ml_dtypes.bfloat16)
    return high, low


def angle_tables(sign):
    index = np.arange(96)
    angles = 2.0 * np.pi * (np.outer(index, index) % 96) / 96
    return np.cos(angles), sign * np.sin(angles)


def lane_table(sign):
    cosine, sine = angle_tables(sign)
    table = np.zeros((256, 256))
    table[:96, :96] = cosine
    table[128:224, 128:224] = cosine
    table[:96, 128:224] = sine
    table[128:224, :96] = -sine
    return split_table(table)


def slab_order():
    part = np.array([0] * 8 + [1] * 8 + [0] * 4 + [1] * 4)
    virtual = np.array(list(range(8)) * 2 + list(range(8, 12)) * 2)
    slot = np.array([0, 0, 0, 0, 1, 1, 1, 1, 0, 0, 1, 1])[virtual]
    local = np.array([0, 1, 2, 3, 0, 1, 2, 3, 4, 5, 4, 5])[virtual]
    planes = np.array([[0, 1, 2, 3, 8, 9], [4, 5, 6, 7, 10, 11]])
    places = [
        slot * 192 + part * 96 + 12 * f + planes[half][local] for half in range(2) for f in range(PARTS)
    ]
    return np.concatenate(places)


def row_tables():
    order = slab_order()
    cosine, sine = angle_tables(-1.0)
    single = np.block([[cosine, -sine], [sine, cosine]])
    forward = np.kron(np.eye(2), single)[:, order]
    cosine, sine = angle_tables(1.0)
    single = np.block([[cosine, -sine], [sine, cosine]])
    inverse = np.kron(np.eye(2), single)[order]
    return split_table(forward) + split_table(inverse)


def const_times(value, angle, count):
    re, im = value
    angle %= count
    if angle == 0:
        return value
    if 2 * angle == count:
        return (-re, -im)
    if 4 * angle == count:
        return (-im, re)
    if 4 * angle == 3 * count:
        return (im, -re)
    c = math.cos(2 * math.pi * angle / count)
    s = math.sin(2 * math.pi * angle / count)
    if (8 * angle) % count == 0:
        r = math.sqrt(0.5)
        c = math.copysign(1.0, c)
        s = math.copysign(1.0, s)
        a = re * (c * r)
        b = im * (c * r)
        return (a - b, a + b) if c == s else (a + b, b - a)
    return (re * c - im * s, re * s + im * c)


def add(a, b):
    return (a[0] + b[0], a[1] + b[1])


def sub(a, b):
    return (a[0] - b[0], a[1] - b[1])


def small_dft(x, sign):
    n = len(x)
    if n == 2:
        return [add(x[0], x[1]), sub(x[0], x[1])]
    if n == 3:
        total = add(x[1], x[2])
        diff = sub(x[1], x[2])
        r = sign * math.sqrt(0.75)
        mid = (x[0][0] - 0.5 * total[0], x[0][1] - 0.5 * total[1])
        turn = (-r * diff[1], r * diff[0])
        return [add(x[0], total), add(mid, turn), sub(mid, turn)]
    if n == 4:
        a, b = add(x[0], x[2]), sub(x[0], x[2])
        c, d = add(x[1], x[3]), sub(x[1], x[3])
        d = const_times(d, sign, 4)
        return [add(a, c), add(b, d), sub(a, c), sub(b, d)]
    inner = 4
    outer = n // inner
    out = [None] * n
    columns = []
    for low in range(outer):
        column = small_dft([x[outer * i + low] for i in range(inner)], sign)
        columns.append([const_times(v, sign * low * k, n) for k, v in enumerate(column)])
    for k in range(inner):
        row = small_dft([columns[low][k] for low in range(outer)], sign)
        for j in range(outer):
            out[k + inner * j] = row[j]
    return out


def leading_dft(field, sign):
    def tile(t, carry):
        rows = pl.ds(pl.multiple_of(t * 8, 8), 8)

        def load(y):
            return (field[y, rows, 0:128], field[y, rows, 128:256])

        def save(y, v):
            field[y, rows, 0:128] = v[0]
            field[y, rows, 128:256] = v[1]

        for low in range(8):
            column = small_dft([load(8 * i + low) for i in range(12)], sign)
            for k, v in enumerate(column):
                save(8 * k + low, const_times(v, sign * low * k, 96))
        return carry

    lax.fori_loop(0, 3, tile, 0, unroll=UNROLL)


def second_pass(field, k, rows, sign):
    values = [
        (field[8 * k + low, rows, 0:128], field[8 * k + low, rows, 128:256]) for low in range(8)
    ]
    return small_dft(values, sign)


def whole_dft(source, target, sign):
    leading_dft(source, sign)

    def tile(t, carry):
        rows = pl.ds(pl.multiple_of(t * 8, 8), 8)
        for k in range(12):
            for j, v in enumerate(second_pass(source, k, rows, sign)):
                target[k + 12 * j, rows, 0:128] = v[0]
                target[k + 12 * j, rows, 128:256] = v[1]
        return carry

    lax.fori_loop(0, 3, tile, 0, unroll=UNROLL)


def lanes():
    return lax.broadcasted_iota(jnp.int32, (8, 128), 1)


def unpack(wide):
    lane = lanes()
    out = []
    for q in range(3):
        a, b, c = (wide[:, 128 * (3 * q + i) : 128 * (3 * q + i + 1)] for i in range(3))
        out.append(a)
        out.append(jnp.where(lane < 32, pltpu.roll(a, 32, 1), pltpu.roll(b, 32, 1)))
        out.append(jnp.where(lane < 64, pltpu.roll(b, 64, 1), pltpu.roll(c, 64, 1)))
        out.append(pltpu.roll(c, 96, 1))
    return out


def pack(tiles):
    lane = lanes()
    out = []
    for q in range(3):
        a, b, c, d = tiles[4 * q : 4 * q + 4]
        b = pltpu.roll(b, 96, 1)
        c = pltpu.roll(c, 64, 1)
        d = pltpu.roll(d, 32, 1)
        out.append(jnp.where(lane < 96, a, b))
        out.append(jnp.where(lane < 64, b, c))
        out.append(jnp.where(lane < 32, c, d))
    return jnp.concatenate(out, axis=1)


def flip(x):
    return pltpu.roll(x, 4, 0)


def top(x):
    return lax.broadcasted_iota(jnp.int32, x.shape, 0) < 4


def split_dot(x, high, low):
    x_high = x.astype(jnp.bfloat16)
    x_low = (x - x_high.astype(jnp.float32)).astype(jnp.bfloat16)
    dot = functools.partial(jnp.dot, preferred_element_type=jnp.float32)
    return dot(x_high, high) + (dot(x_high, low) + dot(x_low, high))


def dot_split(high, low, x):
    x_high = x.astype(jnp.bfloat16)
    x_low = (x - x_high.astype(jnp.float32)).astype(jnp.bfloat16)
    dot = functools.partial(jnp.dot, preferred_element_type=jnp.float32)
    return dot(high, x_high) + (dot(low, x_high) + dot(high, x_low))


def row_index(x):
    return lax.broadcasted_iota(jnp.int32, x.shape, 0)


def combine(a0, a1, b0, b1):
    upper = top(a0)
    row = row_index(b0)
    rest = jnp.where(
        row < 2,
        b0,
        jnp.where(
            row < 4,
            pltpu.roll(b1, 2, 0),
            jnp.where(row < 6, pltpu.roll(b0, 2, 0), pltpu.roll(b1, 4, 0)),
        ),
    )
    return jnp.where(upper, a0, flip(a1)), jnp.where(upper, flip(a0), a1), rest


def split(t0, t1, t2):
    upper = top(t0)
    low = row_index(t2) < 2
    back = pltpu.roll(t2, 6, 0)
    return (
        jnp.where(upper, t0, flip(t1)),
        jnp.where(upper, flip(t0), t1),
        jnp.where(low, t2, back),
        jnp.where(low, back, flip(t2)),
    )


def list_load(ref, start):
    x = ref[pl.ds(pl.multiple_of(start, 8), 72), :]
    return jnp.concatenate([x[8 * i : 8 * i + 8] for i in range(9)], axis=1)


def list_save(ref, start, x):
    for i in range(9):
        ref[pl.ds(pl.multiple_of(start + 8 * i, 8), 8), :] = x[:, 128 * i : 128 * i + 128]


def second_start(g):
    return 8 * (72 + 9 * lax.rem(g, 4))


def half_load(ref, g):
    b = list_load(ref, second_start(g))
    return list_load(ref, 72 * g), jnp.where(g >= 4, flip(b), b)


def half_save(ref, g, a, b):
    list_save(ref, 72 * g, a)
    old = list_load(ref, second_start(g))
    upper = top(b)
    b = jnp.where(upper, b, flip(b))
    b = jnp.where(g < 4, jnp.where(upper, b, old), jnp.where(upper, old, b))
    list_save(ref, second_start(g), b)


def block_columns(g):
    return pl.ds(pl.multiple_of(g * BLOCK, 128), BLOCK)


def slab_rows(ref, g):
    cols = block_columns(g)
    rest = jnp.concatenate([ref[0, 8:12, cols], ref[1, 8:12, cols]], axis=0)
    return ref[0, 0:8, cols], ref[1, 0:8, cols], rest


def orbital_rows(ref, g):
    cols = block_columns(g)
    return ref[0:8, cols], ref[8:16, cols], ref[16:24, cols]


def halves_kernel(place, orbital, keep, send):
    first = place[2] == 0

    def block(g, carry):
        a0, a1, b0, b1 = split(*slab_rows(orbital, g))
        half_save(keep, g, jnp.where(first, a0, a1), jnp.where(first, b0, b1))
        half_save(send, g, jnp.where(first, a1, a0), jnp.where(first, b1, b0))
        return carry

    lax.fori_loop(0, PARTS, block, 0, unroll=UNROLL)
    for ref in (keep, send):
        ref[TILES:LIST, :] = jnp.zeros((LIST - TILES, 128), jnp.float32)


def assemble_kernel(place, keep, recv, keep_other, recv_other, mine, other):
    first = place[2] == 0

    def block(g, carry):
        cols = block_columns(g)
        for own, far, out in ((keep, recv, mine), (keep_other, recv_other, other)):
            (a0, b0), (a1, b1) = half_load(own, g), half_load(far, g)
            rows = combine(
                jnp.where(first, a0, a1),
                jnp.where(first, a1, a0),
                jnp.where(first, b0, b1),
                jnp.where(first, b1, b0),
            )
            for r in range(3):
                out[8 * r : 8 * r + 8, cols] = rows[r]
        return carry

    lax.fori_loop(0, PARTS, block, 0, unroll=UNROLL)


def applied_kernel(place, near, got, far, out):
    first = place[2] == 0

    def block(g, carry):
        cols = block_columns(g)
        a0, b0 = half_load(near, g)
        a1, b1 = half_load(got, g)
        a0, b0 = a0 + a1, b0 + b1
        a1, b1 = half_load(far, g)
        t0, t1, t2 = combine(
            jnp.where(first, a0, a1),
            jnp.where(first, a1, a0),
            jnp.where(first, b0, b1),
            jnp.where(first, b1, b0),
        )
        for part, rows, rest in ((0, t0, t2[0:4]), (1, t1, t2[4:8])):
            for x in range(12):
                row = rows[x : x + 1] if x < 8 else rest[x - 8 : x - 7]
                out[x, part : part + 1, cols] = row
        return carry

    lax.fori_loop(0, PARTS, block, 0, unroll=UNROLL)


def served_rows(ref, g):
    a, b = half_load(ref, g)
    return combine(a, a, b, b)


def forward_kernel(place, served, mine, other, table, out, line, field, spectrum):
    def block(g, carry):
        s0, s1, s2 = served_rows(served, g)
        parts = []
        rests = []
        for ref in (mine, other):
            re, im, rest = orbital_rows(ref, g)
            parts.append((s0 * re + s1 * im, s0 * im - s1 * re))
            same = s2 * rest
            cross = s2 * flip(rest)
            rests.append((same + flip(same), cross - flip(cross)))
        upper = top(s2)
        parts.append(
            (jnp.where(upper, rests[0][0], rests[1][0]), jnp.where(upper, rests[0][1], -rests[1][1]))
        )
        for t, (re, im) in enumerate(parts):
            for y, (a, b) in enumerate(zip(unpack(re), unpack(im))):
                line[24 * y + 8 * t : 24 * y + 8 * t + 8, 0:128] = a
                line[24 * y + 8 * t : 24 * y + 8 * t + 8, 128:256] = b
        result = split_dot(line[...], table[0:256], table[256:512])
        field[pl.ds(g * 12, 12)] = result.reshape(12, 24, 256)
        return carry

    lax.fori_loop(0, PARTS, block, 0, unroll=UNROLL)
    whole_dft(field, spectrum, -1)

    def send(g, carry):
        packed = []
        for t in range(3):
            rows = slice(8 * t, 8 * t + 8)
            packed.append(
                tuple(
                    pack([spectrum[g * 12 + y, rows, c : c + 128] for y in range(12)])
                    for c in (0, 128)
                )
            )
        re, im = packed[2]
        upper = top(re)
        for p, rest in enumerate(
            (jnp.where(upper, re, flip(im)), jnp.where(upper, flip(re), im))
        ):
            out[p, g, 0:8, :] = packed[p][0]
            out[p, g, 8:16, :] = packed[p][1]
            out[p, g, 16:24, :] = rest
        return carry

    lax.fori_loop(0, PARTS, send, 0, unroll=UNROLL)


def column_kernel(blocks, coulomb, tables, out):
    width = BLOCK // 3
    for i in range(3):
        cols = slice(width * i, width * i + width)
        x = blocks[:, :, cols].reshape(16 * ROWS, width)
        x = dot_split(tables[0:384], tables[384:768], x)
        k = coulomb[:, cols]
        x = jnp.concatenate([x[96 * j : 96 * j + 96] * k for j in range(4)], axis=0)
        x = dot_split(tables[768:1152], tables[1152:1536], x)
        out[:, :, cols] = x.reshape(16, ROWS, width)


def backward_kernel(
    place, blocks, served, mine, other, table, own_near, own_far, away_near, away_far, terms,
    line, field, spectrum, total,
):
    first = place[2] == 0

    def receive(g, carry):
        rests = [blocks[p, g, 16:24, :] for p in range(2)]
        upper = top(rests[0])
        parts = [(blocks[p, g, 0:8, :], blocks[p, g, 8:16, :]) for p in range(2)]
        parts.append(
            (
                jnp.where(upper, rests[0], flip(rests[1])),
                jnp.where(upper, flip(rests[0]), rests[1]),
            )
        )
        for t, (re, im) in enumerate(parts):
            rows = slice(8 * t, 8 * t + 8)
            for y, (a, b) in enumerate(zip(unpack(re), unpack(im))):
                spectrum[g * 12 + y, rows, 0:128] = a
                spectrum[g * 12 + y, rows, 128:256] = b
        return carry

    lax.fori_loop(0, PARTS, receive, 0, unroll=UNROLL)
    whole_dft(spectrum, field, 1)

    def block(g, carry):
        x = field[pl.ds(g * 12, 12)].reshape(288, 256)
        line[...] = split_dot(x, table[0:256], table[256:512])
        packed = []
        for t in range(3):
            packed.append(
                tuple(
                    pack([line[24 * y + 8 * t : 24 * y + 8 * t + 8, c : c + 128] for y in range(12)])
                    for c in (0, 128)
                )
            )
        re, im = packed[2]
        upper = top(re)
        rests = (jnp.where(upper, re, flip(im)), jnp.where(upper, flip(re), im))
        s0, s1, s2 = served_rows(served, g)
        sums = None
        for p, (ref, near, far) in enumerate(
            ((mine, own_near, own_far), (other, away_near, away_far))
        ):
            vr, vi = packed[p]
            v2 = rests[p]
            same = s2 * v2
            cross = s2 * flip(v2)
            a0, a1, b0, b1 = split(
                s0 * vr - s1 * vi,
                s0 * vi + s1 * vr,
                jnp.where(upper, same - flip(same), cross + flip(cross)),
            )
            half_save(near, g, jnp.where(first, a0, a1), jnp.where(first, b0, b1))
            half_save(far, g, jnp.where(first, a1, a0), jnp.where(first, b1, b0))
            ore, oim, rest = orbital_rows(ref, g)
            same = v2 * rest
            cross = v2 * flip(rest)
            turned = flip(cross)
            both = (
                vr * ore + vi * oim,
                vr * oim - vi * ore,
                jnp.where(upper, same + flip(same), turned - cross),
            )
            sums = both if sums is None else tuple(a + b for a, b in zip(sums, both))
        a0, a1, b0, b1 = split(*sums)
        half_save(total, g, a0 + a1, b0 + b1)
        return carry

    lax.fori_loop(0, PARTS, block, 0, unroll=UNROLL)
    lane = lanes()

    def tile(l):
        return total[8 * l : 8 * l + 8, :]

    def turn(x):
        return pltpu.roll(x, 64, 1)

    for g in range(4):
        middle = 9 * g + 4
        for odd in range(2):
            begin = 9 * g + 5 * odd
            tiles = [tile(begin + i) for i in range(4)] + [tile(begin + 36 + i) for i in range(4)]
            a, b = tile(middle), tile(middle + 36)
            a, b = (turn(a), b) if odd else (a, turn(b))
            tiles.append(jnp.where(lane < 64, a, b))
            tiles += [tile(72 + begin + i) for i in range(4)]
            a = tile(72 + middle)
            tiles.append(turn(a) if odd else a)
            for i, x in enumerate(tiles):
                start = (2 * g + odd) * CHUNK + 8 * i
                terms[start : start + 8, :] = x


def finish_kernel(place, blocks, *pieces):
    lane = lanes()
    second_core = place[0] == 1
    odd = place[1] == 1
    second_half = place[2] == 1
    tiles = []
    for i in range(14):
        x = [blocks[CHUNK * q + 8 * i : CHUNK * q + 8 * i + 8, :] for q in range(8)]
        while len(x) > 1:
            x = [x[2 * j] + x[2 * j + 1] for j in range(len(x) // 2)]
        tiles.append(x[0])

    def widen(f, h):
        s = [pltpu.roll(x, 64, 1) for x in f]
        wide = [
            jnp.where(odd, jnp.where(lane < 64, a, b), c)
            for a, b, c in zip([h] + s, s + [s[3]], f + [h])
        ]
        s = [pltpu.roll(x, 96, 1) for x in wide[2:]]
        second = [jnp.where(lane < 96, s[0], s[1]), jnp.where(lane < 96, s[1], s[2]), s[2]]
        return wide[:3], second

    left = widen(tiles[0:4], tiles[8])
    right = widen(tiles[4:8], pltpu.roll(tiles[8], 64, 1))
    rest = widen(tiles[9:13], tiles[13])
    for piece, out in enumerate(pieces):
        half = second_half if piece < 2 else jnp.logical_not(second_half)
        core = second_core if piece % 2 == 0 else jnp.logical_not(second_core)
        for i in range(3):
            x = [jnp.where(core, y[1][i], y[0][i]) for y in (left, right, rest)]
            a = jnp.where(half, x[1], x[0])
            b = jnp.where(half, flip(x[2]), x[2])
            width = 128 if i < 2 else 32
            cols = slice(128 * i, 128 * i + width)
            out[0:8, cols] = a[:, :width]
            out[8:12, cols] = b[0:4, :width]


def serving_kernel(place, p00, p01, p10, p11, out):
    second_core = place[0] == 1
    second_half = place[2] == 1
    x = [[p00[...], p01[...]], [p10[...], p11[...]]]
    for member in range(2):
        swap = second_core if member == 0 else jnp.logical_not(second_core)
        near, far = (jnp.where(swap, x[i][1], x[i][0]) for i in range(2))
        h0 = jnp.where(second_half, far, near)
        h1 = jnp.where(second_half, near, far)
        for part in range(2):
            for i in range(12):
                source = h0 if i in (0, 1, 2, 3, 8, 9) else h1
                j = i % 4 + 4 * part if i < 8 else 8 + i % 2 + 2 * part
                out[member, i, part : part + 1, :] = source[j : j + 1]


def f32(*shape):
    return jax.ShapeDtypeStruct(shape, jnp.float32)


def shards(orbitals, serve_order):
    rank_fft = lax.axis_index("fft")
    rank_band = lax.axis_index("band")
    core = rank_band % 2
    line = rank_band // 2 % 8
    half = rank_band // 16
    place = jnp.stack([core, line % 2, half]).astype(jnp.int32)
    z_groups = [[y * 16 + 2 * z + c for z in range(8)] for y in range(2) for c in range(2)]
    plane_groups = [
        [(y * 16 + b) * PARTS + f for y in range(2) for f in range(PARTS)] for b in range(16)
    ]
    scale = -mixing / (NX * NY * NZ)

    coulomb = kernel_columns(rank_fft * 12, 12) * scale
    params = pltpu.CompilerParams(vmem_limit_bytes=VMEM)
    scalars = pl.BlockSpec(memory_space=pltpu.SMEM)
    whole = pl.BlockSpec(memory_space=pltpu.VMEM)

    def call(kernel, shapes, inputs, scratch=()):
        return pl.pallas_call(
            kernel,
            out_shape=shapes,
            in_specs=[scalars] + [whole] * len(inputs),
            out_specs=jax.tree.map(lambda _: whole, shapes),
            scratch_shapes=list(scratch),
            compiler_params=params,
        )(place, *inputs)

    def swap(x, bits):
        return lax.ppermute(x, "band", [(i, i ^ bits) for i in range(32)])

    def line_exchange(blocks):
        return lax.all_to_all(blocks, "band", 0, 0, axis_index_groups=z_groups, tiled=True)

    def plane_exchange(blocks):
        return lax.all_to_all(
            blocks, ("band", "fft"), 0, 0, axis_index_groups=plane_groups, tiled=True
        )

    lists = f32(LIST, 128)
    keep, send = call(halves_kernel, (lists, lists), (orbitals.reshape(2, 12, PLANE),))
    recv = swap(send, 16)
    keep_other = swap(keep, 1)
    recv_other = swap(recv, 1)
    serving = serve_order[core]
    near = serving // 16 == half
    same = serving % 2 == core
    candidate = jnp.where(
        same, jnp.where(near, keep, recv), jnp.where(near, keep_other, recv_other)
    )
    blocks = line_exchange(candidate.reshape(8, CHUNK, 128))
    block = lax.dynamic_index_in_dim(blocks, serving // 2 % 8, 0, keepdims=True)
    rows = f32(ROWS, PLANE)
    mine, other = call(assemble_kernel, (rows, rows), (keep, recv, keep_other, recv_other))
    block, coulomb, mine, other = lax.optimization_barrier((block, coulomb, mine, other))
    served = line_exchange(jnp.broadcast_to(block, blocks.shape)).reshape(LIST, 128)

    scratch = [
        pltpu.VMEM((288, 256), jnp.float32),
        pltpu.VMEM((NY, ROWS, 256), jnp.float32),
        pltpu.VMEM((NY, ROWS, 256), jnp.float32),
    ]
    table = jnp.asarray(np.concatenate(lane_table(-1.0)))
    blocks = call(
        forward_kernel, f32(2, PARTS, ROWS, BLOCK), (served, mine, other, table), scratch
    )
    blocks = plane_exchange(blocks.reshape(16, ROWS, BLOCK))
    tables = jnp.asarray(np.concatenate(row_tables()))
    blocks = pl.pallas_call(
        column_kernel,
        out_shape=f32(16, ROWS, BLOCK),
        in_specs=[whole] * 3,
        out_specs=whole,
        compiler_params=params,
    )(blocks, coulomb, tables)
    blocks = plane_exchange(blocks).reshape(2, PARTS, ROWS, BLOCK)
    table = jnp.asarray(np.concatenate(lane_table(1.0)))
    short = f32(TILES, 128)
    own_near, own_far, away_near, away_far, terms = call(
        backward_kernel,
        (short, short, short, short, lists),
        (blocks, served, mine, other, table),
        scratch + [pltpu.VMEM((TILES, 128), jnp.float32)],
    )
    far = swap(own_far + swap(away_far, 1), 16)
    got = swap(away_near, 1)
    applied = call(applied_kernel, f32(12, 2, PLANE), (own_near, got, far))
    blocks = line_exchange(terms.reshape(8, CHUNK, 128)).reshape(LIST, 128)
    blocks, applied = lax.optimization_barrier((blocks, applied))
    small = f32(12, HALF)
    pieces = call(finish_kernel, (small,) * 4, (blocks,))
    pieces = [pieces[0], swap(pieces[1], 1), swap(pieces[2], 16), swap(pieces[3], 17)]
    serving_exchange = call(serving_kernel, f32(SERVE, 12, 2, HALF), pieces)
    return (applied.transpose(1, 0, 2)[None], serving_exchange.transpose(0, 2, 1, 3))


def solution(mesh):
    return jax.shard_map(
        shards,
        mesh=mesh,
        in_specs=(P("band", None, "fft", None), P()),
        out_specs=(P("band", None, "fft", None), P(None, None, "fft", "band")),
        check_vma=False,
    )
```

```python
import functools
import math

import jax
import jax.numpy as jnp
import ml_dtypes
import numpy as np
from jax import lax
from jax.experimental import pallas as pl
from jax.experimental.pallas import tpu as pltpu
from jax.sharding import PartitionSpec as P

NX = 96
NY = 96
NZ = 96
SERVE = 2
CHIPS = 16
PARTS = 8
ROWS = 24
PLANE = NY * NZ
BLOCK = PLANE // PARTS
CHUNK = 112
LIST = 8 * CHUNK
TILES = 108 * 8
HALF = PLANE // CHIPS // 2
UNROLL = True
VMEM = 48 * 1024 * 1024

cell_side = 41.04
mixing = 0.25


def frequencies(count):
    signed = (jnp.arange(count, dtype=jnp.int32) + count // 2) % count - count // 2
    return signed.astype(jnp.float32) * (2.0 * math.pi / cell_side)


def kernel_columns(start, width):
    freq_x = frequencies(NX)
    freq_y = lax.dynamic_slice_in_dim(frequencies(NY), start, width)
    freq_z = frequencies(NZ)
    freq_y = jnp.broadcast_to(freq_y[:, None], (width, NZ)).reshape(-1)
    freq_z = jnp.broadcast_to(freq_z[None], (width, NZ)).reshape(-1)
    squared = freq_x[:, None] ** 2 + freq_y[None] ** 2 + freq_z[None] ** 2
    radius = cell_side * (3.0 / (4.0 * math.pi)) ** (1.0 / 3.0)
    safe_square = jnp.where(squared > 0, squared, 1.0)
    general = 4.0 * math.pi * (1.0 - jnp.cos(jnp.sqrt(safe_square) * radius)) / safe_square
    return jnp.where(squared > 0, general, 2.0 * math.pi * radius * radius)


def split_table(table):
    high = table.astype(ml_dtypes.bfloat16)
    low = (table - high.astype(np.float64)).astype(ml_dtypes.bfloat16)
    return high, low


def angle_tables(sign):
    index = np.arange(96)
    angles = 2.0 * np.pi * (np.outer(index, index) % 96) / 96
    return np.cos(angles), sign * np.sin(angles)


def lane_table(sign):
    cosine, sine = angle_tables(sign)
    table = np.zeros((256, 256))
    table[:96, :96] = cosine
    table[128:224, 128:224] = cosine
    table[:96, 128:224] = sine
    table[128:224, :96] = -sine
    return split_table(table)


def slab_order():
    part = np.array([0] * 8 + [1] * 8 + [0] * 4 + [1] * 4)
    virtual = np.array(list(range(8)) * 2 + list(range(8, 12)) * 2)
    slot = np.array([0, 0, 0, 0, 1, 1, 1, 1, 0, 0, 1, 1])[virtual]
    local = np.array([0, 1, 2, 3, 0, 1, 2, 3, 4, 5, 4, 5])[virtual]
    planes = np.array([[0, 1, 2, 3, 8, 9], [4, 5, 6, 7, 10, 11]])
    places = [
        slot * 192 + part * 96 + 12 * f + planes[half][local] for half in range(2) for f in range(PARTS)
    ]
    return np.concatenate(places)


def row_tables():
    order = slab_order()
    cosine, sine = angle_tables(-1.0)
    single = np.block([[cosine, -sine], [sine, cosine]])
    forward = np.kron(np.eye(2), single)[:, order]
    cosine, sine = angle_tables(1.0)
    single = np.block([[cosine, -sine], [sine, cosine]])
    inverse = np.kron(np.eye(2), single)[order]
    return split_table(forward) + split_table(inverse)


def const_times(value, angle, count):
    re, im = value
    angle %= count
    if angle == 0:
        return value
    if 2 * angle == count:
        return (-re, -im)
    if 4 * angle == count:
        return (-im, re)
    if 4 * angle == 3 * count:
        return (im, -re)
    c = math.cos(2 * math.pi * angle / count)
    s = math.sin(2 * math.pi * angle / count)
    if (8 * angle) % count == 0:
        r = math.sqrt(0.5)
        c = math.copysign(1.0, c)
        s = math.copysign(1.0, s)
        a = re * (c * r)
        b = im * (c * r)
        return (a - b, a + b) if c == s else (a + b, b - a)
    return (re * c - im * s, re * s + im * c)


def add(a, b):
    return (a[0] + b[0], a[1] + b[1])


def sub(a, b):
    return (a[0] - b[0], a[1] - b[1])


def small_dft(x, sign):
    n = len(x)
    if n == 2:
        return [add(x[0], x[1]), sub(x[0], x[1])]
    if n == 3:
        total = add(x[1], x[2])
        diff = sub(x[1], x[2])
        r = sign * math.sqrt(0.75)
        mid = (x[0][0] - 0.5 * total[0], x[0][1] - 0.5 * total[1])
        turn = (-r * diff[1], r * diff[0])
        return [add(x[0], total), add(mid, turn), sub(mid, turn)]
    if n == 4:
        a, b = add(x[0], x[2]), sub(x[0], x[2])
        c, d = add(x[1], x[3]), sub(x[1], x[3])
        d = const_times(d, sign, 4)
        return [add(a, c), add(b, d), sub(a, c), sub(b, d)]
    inner = 4
    outer = n // inner
    out = [None] * n
    columns = []
    for low in range(outer):
        column = small_dft([x[outer * i + low] for i in range(inner)], sign)
        columns.append([const_times(v, sign * low * k, n) for k, v in enumerate(column)])
    for k in range(inner):
        row = small_dft([columns[low][k] for low in range(outer)], sign)
        for j in range(outer):
            out[k + inner * j] = row[j]
    return out


def leading_dft(field, sign):
    def tile(t, carry):
        rows = pl.ds(pl.multiple_of(t * 8, 8), 8)

        def load(y):
            return (field[y, rows, 0:128], field[y, rows, 128:256])

        def save(y, v):
            field[y, rows, 0:128] = v[0]
            field[y, rows, 128:256] = v[1]

        for low in range(8):
            column = small_dft([load(8 * i + low) for i in range(12)], sign)
            for k, v in enumerate(column):
                save(8 * k + low, const_times(v, sign * low * k, 96))
        return carry

    lax.fori_loop(0, 3, tile, 0, unroll=UNROLL)


def second_pass(field, k, rows, sign):
    values = [
        (field[8 * k + low, rows, 0:128], field[8 * k + low, rows, 128:256]) for low in range(8)
    ]
    return small_dft(values, sign)


def whole_dft(source, target, sign):
    leading_dft(source, sign)

    def tile(t, carry):
        rows = pl.ds(pl.multiple_of(t * 8, 8), 8)
        for k in range(12):
            for j, v in enumerate(second_pass(source, k, rows, sign)):
                target[k + 12 * j, rows, 0:128] = v[0]
                target[k + 12 * j, rows, 128:256] = v[1]
        return carry

    lax.fori_loop(0, 3, tile, 0, unroll=UNROLL)


def lanes():
    return lax.broadcasted_iota(jnp.int32, (8, 128), 1)


def unpack(wide):
    lane = lanes()
    out = []
    for q in range(3):
        a, b, c = (wide[:, 128 * (3 * q + i) : 128 * (3 * q + i + 1)] for i in range(3))
        out.append(a)
        out.append(jnp.where(lane < 32, pltpu.roll(a, 32, 1), pltpu.roll(b, 32, 1)))
        out.append(jnp.where(lane < 64, pltpu.roll(b, 64, 1), pltpu.roll(c, 64, 1)))
        out.append(pltpu.roll(c, 96, 1))
    return out


def pack(tiles):
    lane = lanes()
    out = []
    for q in range(3):
        a, b, c, d = tiles[4 * q : 4 * q + 4]
        b = pltpu.roll(b, 96, 1)
        c = pltpu.roll(c, 64, 1)
        d = pltpu.roll(d, 32, 1)
        out.append(jnp.where(lane < 96, a, b))
        out.append(jnp.where(lane < 64, b, c))
        out.append(jnp.where(lane < 32, c, d))
    return jnp.concatenate(out, axis=1)


def flip(x):
    return pltpu.roll(x, 4, 0)


def top(x):
    return lax.broadcasted_iota(jnp.int32, x.shape, 0) < 4


def split_dot(x, high, low):
    x_high = x.astype(jnp.bfloat16)
    x_low = (x - x_high.astype(jnp.float32)).astype(jnp.bfloat16)
    dot = functools.partial(jnp.dot, preferred_element_type=jnp.float32)
    return dot(x_high, high) + (dot(x_high, low) + dot(x_low, high))


def dot_split(high, low, x):
    x_high = x.astype(jnp.bfloat16)
    x_low = (x - x_high.astype(jnp.float32)).astype(jnp.bfloat16)
    dot = functools.partial(jnp.dot, preferred_element_type=jnp.float32)
    return dot(high, x_high) + (dot(low, x_high) + dot(high, x_low))


def row_index(x):
    return lax.broadcasted_iota(jnp.int32, x.shape, 0)


def combine(a0, a1, b0, b1):
    upper = top(a0)
    row = row_index(b0)
    rest = jnp.where(
        row < 2,
        b0,
        jnp.where(
            row < 4,
            pltpu.roll(b1, 2, 0),
            jnp.where(row < 6, pltpu.roll(b0, 2, 0), pltpu.roll(b1, 4, 0)),
        ),
    )
    return jnp.where(upper, a0, flip(a1)), jnp.where(upper, flip(a0), a1), rest


def split(t0, t1, t2):
    upper = top(t0)
    low = row_index(t2) < 2
    back = pltpu.roll(t2, 6, 0)
    return (
        jnp.where(upper, t0, flip(t1)),
        jnp.where(upper, flip(t0), t1),
        jnp.where(low, t2, back),
        jnp.where(low, back, flip(t2)),
    )


def list_load(ref, start):
    x = ref[pl.ds(pl.multiple_of(start, 8), 72), :]
    return jnp.concatenate([x[8 * i : 8 * i + 8] for i in range(9)], axis=1)


def list_save(ref, start, x):
    for i in range(9):
        ref[pl.ds(pl.multiple_of(start + 8 * i, 8), 8), :] = x[:, 128 * i : 128 * i + 128]


def second_start(g):
    return 8 * (72 + 9 * lax.rem(g, 4))


def half_load(ref, g):
    b = list_load(ref, second_start(g))
    return list_load(ref, 72 * g), jnp.where(g >= 4, flip(b), b)


def half_save(ref, g, a, b):
    list_save(ref, 72 * g, a)
    old = list_load(ref, second_start(g))
    upper = top(b)
    b = jnp.where(upper, b, flip(b))
    b = jnp.where(g < 4, jnp.where(upper, b, old), jnp.where(upper, old, b))
    list_save(ref, second_start(g), b)


def block_columns(g):
    return pl.ds(pl.multiple_of(g * BLOCK, 128), BLOCK)


def slab_rows(ref, g):
    cols = block_columns(g)
    rest = jnp.concatenate([ref[0, 8:12, cols], ref[1, 8:12, cols]], axis=0)
    return ref[0, 0:8, cols], ref[1, 0:8, cols], rest


def orbital_rows(ref, g):
    cols = block_columns(g)
    return ref[0:8, cols], ref[8:16, cols], ref[16:24, cols]


def halves_kernel(place, orbital, keep, send):
    first = place[2] == 0

    def block(g, carry):
        a0, a1, b0, b1 = split(*slab_rows(orbital, g))
        half_save(keep, g, jnp.where(first, a0, a1), jnp.where(first, b0, b1))
        half_save(send, g, jnp.where(first, a1, a0), jnp.where(first, b1, b0))
        return carry

    lax.fori_loop(0, PARTS, block, 0, unroll=UNROLL)
    for ref in (keep, send):
        ref[TILES:LIST, :] = jnp.zeros((LIST - TILES, 128), jnp.float32)


def applied_kernel(place, near, got, far, out):
    first = place[2] == 0

    def block(g, carry):
        cols = block_columns(g)
        a0, b0 = half_load(near, g)
        a1, b1 = half_load(got, g)
        a0, b0 = a0 + a1, b0 + b1
        a1, b1 = half_load(far, g)
        t0, t1, t2 = combine(
            jnp.where(first, a0, a1),
            jnp.where(first, a1, a0),
            jnp.where(first, b0, b1),
            jnp.where(first, b1, b0),
        )
        for part, rows, rest in ((0, t0, t2[0:4]), (1, t1, t2[4:8])):
            for x in range(12):
                row = rows[x : x + 1] if x < 8 else rest[x - 8 : x - 7]
                out[x, part : part + 1, cols] = row
        return carry

    lax.fori_loop(0, PARTS, block, 0, unroll=UNROLL)


def served_rows(ref, g):
    a, b = half_load(ref, g)
    return combine(a, a, b, b)


def forward_kernel(
    place, served, keep, recv, keep_other, recv_other, table, out, mine, other, line, field, spectrum
):
    first = place[2] == 0

    def block(g, carry):
        s0, s1, s2 = served_rows(served, g)
        parts = []
        rests = []
        cols = block_columns(g)
        for own, far, ref in ((keep, recv, mine), (keep_other, recv_other, other)):
            (a0, b0), (a1, b1) = half_load(own, g), half_load(far, g)
            re, im, rest = combine(
                jnp.where(first, a0, a1),
                jnp.where(first, a1, a0),
                jnp.where(first, b0, b1),
                jnp.where(first, b1, b0),
            )
            for r, rows in enumerate((re, im, rest)):
                ref[8 * r : 8 * r + 8, cols] = rows
            parts.append((s0 * re + s1 * im, s0 * im - s1 * re))
            same = s2 * rest
            cross = s2 * flip(rest)
            rests.append((same + flip(same), cross - flip(cross)))
        upper = top(s2)
        parts.append(
            (jnp.where(upper, rests[0][0], rests[1][0]), jnp.where(upper, rests[0][1], -rests[1][1]))
        )
        for t, (re, im) in enumerate(parts):
            for y, (a, b) in enumerate(zip(unpack(re), unpack(im))):
                line[24 * y + 8 * t : 24 * y + 8 * t + 8, 0:128] = a
                line[24 * y + 8 * t : 24 * y + 8 * t + 8, 128:256] = b
        result = split_dot(line[...], table[0:256], table[256:512])
        field[pl.ds(g * 12, 12)] = result.reshape(12, 24, 256)
        return carry

    lax.fori_loop(0, PARTS, block, 0, unroll=UNROLL)
    whole_dft(field, spectrum, -1)

    def send(g, carry):
        packed = []
        for t in range(3):
            rows = slice(8 * t, 8 * t + 8)
            packed.append(
                tuple(
                    pack([spectrum[g * 12 + y, rows, c : c + 128] for y in range(12)])
                    for c in (0, 128)
                )
            )
        re, im = packed[2]
        upper = top(re)
        for p, rest in enumerate(
            (jnp.where(upper, re, flip(im)), jnp.where(upper, flip(re), im))
        ):
            out[p, g, 0:8, :] = packed[p][0]
            out[p, g, 8:16, :] = packed[p][1]
            out[p, g, 16:24, :] = rest
        return carry

    lax.fori_loop(0, PARTS, send, 0, unroll=UNROLL)


def column_kernel(blocks, coulomb, tables, out):
    width = BLOCK // 3
    for i in range(3):
        cols = slice(width * i, width * i + width)
        x = blocks[:, :, cols].reshape(16 * ROWS, width)
        x = dot_split(tables[0:384], tables[384:768], x)
        k = coulomb[:, cols]
        x = jnp.concatenate([x[96 * j : 96 * j + 96] * k for j in range(4)], axis=0)
        x = dot_split(tables[768:1152], tables[1152:1536], x)
        out[:, :, cols] = x.reshape(16, ROWS, width)


def backward_kernel(
    place, blocks, served, mine, other, table, own_near, own_far, away_near, away_far, terms,
    line, field, spectrum, total,
):
    first = place[2] == 0

    def receive(g, carry):
        rests = [blocks[p, g, 16:24, :] for p in range(2)]
        upper = top(rests[0])
        parts = [(blocks[p, g, 0:8, :], blocks[p, g, 8:16, :]) for p in range(2)]
        parts.append(
            (
                jnp.where(upper, rests[0], flip(rests[1])),
                jnp.where(upper, flip(rests[0]), rests[1]),
            )
        )
        for t, (re, im) in enumerate(parts):
            rows = slice(8 * t, 8 * t + 8)
            for y, (a, b) in enumerate(zip(unpack(re), unpack(im))):
                spectrum[g * 12 + y, rows, 0:128] = a
                spectrum[g * 12 + y, rows, 128:256] = b
        return carry

    lax.fori_loop(0, PARTS, receive, 0, unroll=UNROLL)
    whole_dft(spectrum, field, 1)

    def block(g, carry):
        x = field[pl.ds(g * 12, 12)].reshape(288, 256)
        line[...] = split_dot(x, table[0:256], table[256:512])
        packed = []
        for t in range(3):
            packed.append(
                tuple(
                    pack([line[24 * y + 8 * t : 24 * y + 8 * t + 8, c : c + 128] for y in range(12)])
                    for c in (0, 128)
                )
            )
        re, im = packed[2]
        upper = top(re)
        rests = (jnp.where(upper, re, flip(im)), jnp.where(upper, flip(re), im))
        s0, s1, s2 = served_rows(served, g)
        sums = None
        for p, (ref, near, far) in enumerate(
            ((mine, own_near, own_far), (other, away_near, away_far))
        ):
            vr, vi = packed[p]
            v2 = rests[p]
            same = s2 * v2
            cross = s2 * flip(v2)
            a0, a1, b0, b1 = split(
                s0 * vr - s1 * vi,
                s0 * vi + s1 * vr,
                jnp.where(upper, same - flip(same), cross + flip(cross)),
            )
            half_save(near, g, jnp.where(first, a0, a1), jnp.where(first, b0, b1))
            half_save(far, g, jnp.where(first, a1, a0), jnp.where(first, b1, b0))
            ore, oim, rest = orbital_rows(ref, g)
            same = v2 * rest
            cross = v2 * flip(rest)
            turned = flip(cross)
            both = (
                vr * ore + vi * oim,
                vr * oim - vi * ore,
                jnp.where(upper, same + flip(same), turned - cross),
            )
            sums = both if sums is None else tuple(a + b for a, b in zip(sums, both))
        a0, a1, b0, b1 = split(*sums)
        half_save(total, g, a0 + a1, b0 + b1)
        return carry

    lax.fori_loop(0, PARTS, block, 0, unroll=UNROLL)
    lane = lanes()

    def tile(l):
        return total[8 * l : 8 * l + 8, :]

    def turn(x):
        return pltpu.roll(x, 64, 1)

    for g in range(4):
        middle = 9 * g + 4
        for odd in range(2):
            begin = 9 * g + 5 * odd
            tiles = [tile(begin + i) for i in range(4)] + [tile(begin + 36 + i) for i in range(4)]
            a, b = tile(middle), tile(middle + 36)
            a, b = (turn(a), b) if odd else (a, turn(b))
            tiles.append(jnp.where(lane < 64, a, b))
            tiles += [tile(72 + begin + i) for i in range(4)]
            a = tile(72 + middle)
            tiles.append(turn(a) if odd else a)
            for i, x in enumerate(tiles):
                start = (2 * g + odd) * CHUNK + 8 * i
                terms[start : start + 8, :] = x


def finish_kernel(place, blocks, *pieces):
    lane = lanes()
    second_core = place[0] == 1
    odd = place[1] == 1
    second_half = place[2] == 1
    tiles = []
    for i in range(14):
        x = [blocks[CHUNK * q + 8 * i : CHUNK * q + 8 * i + 8, :] for q in range(8)]
        while len(x) > 1:
            x = [x[2 * j] + x[2 * j + 1] for j in range(len(x) // 2)]
        tiles.append(x[0])

    def widen(f, h):
        s = [pltpu.roll(x, 64, 1) for x in f]
        wide = [
            jnp.where(odd, jnp.where(lane < 64, a, b), c)
            for a, b, c in zip([h] + s, s + [s[3]], f + [h])
        ]
        s = [pltpu.roll(x, 96, 1) for x in wide[2:]]
        second = [jnp.where(lane < 96, s[0], s[1]), jnp.where(lane < 96, s[1], s[2]), s[2]]
        return wide[:3], second

    left = widen(tiles[0:4], tiles[8])
    right = widen(tiles[4:8], pltpu.roll(tiles[8], 64, 1))
    rest = widen(tiles[9:13], tiles[13])
    for piece, out in enumerate(pieces):
        half = second_half if piece < 2 else jnp.logical_not(second_half)
        core = second_core if piece % 2 == 0 else jnp.logical_not(second_core)
        for i in range(3):
            x = [jnp.where(core, y[1][i], y[0][i]) for y in (left, right, rest)]
            a = jnp.where(half, x[1], x[0])
            b = jnp.where(half, flip(x[2]), x[2])
            width = 128 if i < 2 else 32
            cols = slice(128 * i, 128 * i + width)
            out[0:8, cols] = a[:, :width]
            out[8:12, cols] = b[0:4, :width]


def serving_kernel(place, p00, p01, p10, p11, out):
    second_core = place[0] == 1
    second_half = place[2] == 1
    x = [[p00[...], p01[...]], [p10[...], p11[...]]]
    for member in range(2):
        swap = second_core if member == 0 else jnp.logical_not(second_core)
        near, far = (jnp.where(swap, x[i][1], x[i][0]) for i in range(2))
        h0 = jnp.where(second_half, far, near)
        h1 = jnp.where(second_half, near, far)
        for part in range(2):
            for i in range(12):
                source = h0 if i in (0, 1, 2, 3, 8, 9) else h1
                j = i % 4 + 4 * part if i < 8 else 8 + i % 2 + 2 * part
                out[member, i, part : part + 1, :] = source[j : j + 1]


def f32(*shape):
    return jax.ShapeDtypeStruct(shape, jnp.float32)


def shards(orbitals, serve_order):
    rank_fft = lax.axis_index("fft")
    rank_band = lax.axis_index("band")
    core = rank_band % 2
    line = rank_band // 2 % 8
    half = rank_band // 16
    place = jnp.stack([core, line % 2, half]).astype(jnp.int32)
    z_groups = [[y * 16 + 2 * z + c for z in range(8)] for y in range(2) for c in range(2)]
    plane_groups = [
        [(y * 16 + b) * PARTS + f for y in range(2) for f in range(PARTS)] for b in range(16)
    ]
    scale = -mixing / (NX * NY * NZ)

    coulomb = kernel_columns(rank_fft * 12, 12) * scale
    params = pltpu.CompilerParams(vmem_limit_bytes=VMEM)
    scalars = pl.BlockSpec(memory_space=pltpu.SMEM)
    whole = pl.BlockSpec(memory_space=pltpu.VMEM)

    def call(kernel, shapes, inputs, scratch=()):
        return pl.pallas_call(
            kernel,
            out_shape=shapes,
            in_specs=[scalars] + [whole] * len(inputs),
            out_specs=jax.tree.map(lambda _: whole, shapes),
            scratch_shapes=list(scratch),
            compiler_params=params,
        )(place, *inputs)

    def swap(x, bits):
        return lax.ppermute(x, "band", [(i, i ^ bits) for i in range(32)])

    def line_exchange(blocks):
        return lax.all_to_all(blocks, "band", 0, 0, axis_index_groups=z_groups, tiled=True)

    def plane_exchange(blocks):
        return lax.all_to_all(
            blocks, ("band", "fft"), 0, 0, axis_index_groups=plane_groups, tiled=True
        )

    lists = f32(LIST, 128)
    keep, send = call(halves_kernel, (lists, lists), (orbitals.reshape(2, 12, PLANE),))
    recv, coulomb = lax.optimization_barrier((swap(send, 16), coulomb))
    keep_other = swap(keep, 1)
    recv_other = swap(recv, 1)
    serving = serve_order[core]
    near = serving // 16 == half
    same = serving % 2 == core
    candidate = jnp.where(
        same, jnp.where(near, keep, recv), jnp.where(near, keep_other, recv_other)
    )
    blocks = line_exchange(candidate.reshape(8, CHUNK, 128))
    block = lax.dynamic_index_in_dim(blocks, serving // 2 % 8, 0, keepdims=True)
    served = line_exchange(jnp.broadcast_to(block, blocks.shape)).reshape(LIST, 128)

    scratch = [
        pltpu.VMEM((288, 256), jnp.float32),
        pltpu.VMEM((NY, ROWS, 256), jnp.float32),
        pltpu.VMEM((NY, ROWS, 256), jnp.float32),
    ]
    table = jnp.asarray(np.concatenate(lane_table(-1.0)))
    rows = f32(ROWS, PLANE)
    blocks, mine, other = call(
        forward_kernel,
        (f32(2, PARTS, ROWS, BLOCK), rows, rows),
        (served, keep, recv, keep_other, recv_other, table),
        scratch,
    )
    blocks = plane_exchange(blocks.reshape(16, ROWS, BLOCK))
    tables = jnp.asarray(np.concatenate(row_tables()))
    blocks = pl.pallas_call(
        column_kernel,
        out_shape=f32(16, ROWS, BLOCK),
        in_specs=[whole] * 3,
        out_specs=whole,
        compiler_params=params,
    )(blocks, coulomb, tables)
    blocks = plane_exchange(blocks).reshape(2, PARTS, ROWS, BLOCK)
    table = jnp.asarray(np.concatenate(lane_table(1.0)))
    short = f32(TILES, 128)
    own_near, own_far, away_near, away_far, terms = call(
        backward_kernel,
        (short, short, short, short, lists),
        (blocks, served, mine, other, table),
        scratch + [pltpu.VMEM((TILES, 128), jnp.float32)],
    )
    far = swap(own_far + swap(away_far, 1), 16)
    got = swap(away_near, 1)
    applied = call(applied_kernel, f32(12, 2, PLANE), (own_near, got, far))
    blocks = line_exchange(terms.reshape(8, CHUNK, 128)).reshape(LIST, 128)
    blocks, applied = lax.optimization_barrier((blocks, applied))
    small = f32(12, HALF)
    pieces = call(finish_kernel, (small,) * 4, (blocks,))
    pieces = [pieces[0], swap(pieces[1], 1), swap(pieces[2], 16), swap(pieces[3], 17)]
    serving_exchange = call(serving_kernel, f32(SERVE, 12, 2, HALF), pieces)
    return (applied.transpose(1, 0, 2)[None], serving_exchange.transpose(0, 2, 1, 3))


def solution(mesh):
    return jax.shard_map(
        shards,
        mesh=mesh,
        in_specs=(P("band", None, "fft", None), P()),
        out_specs=(P("band", None, "fft", None), P(None, None, "fft", "band")),
        check_vma=False,
    )
```

```python
import functools
import math

import jax
import jax.numpy as jnp
import ml_dtypes
import numpy as np
from jax import lax
from jax.experimental import pallas as pl
from jax.experimental.pallas import tpu as pltpu
from jax.sharding import PartitionSpec as P

NX = 96
NY = 96
NZ = 96
SERVE = 2
CHIPS = 16
PARTS = 8
ROWS = 24
PLANE = NY * NZ
BLOCK = PLANE // PARTS
CHUNK = 112
LIST = 8 * CHUNK
TILES = 108 * 8
HALF = PLANE // CHIPS // 2
UNROLL = True
VMEM = 48 * 1024 * 1024

cell_side = 41.04
mixing = 0.25


def frequencies(count):
    signed = (jnp.arange(count, dtype=jnp.int32) + count // 2) % count - count // 2
    return signed.astype(jnp.float32) * (2.0 * math.pi / cell_side)


def kernel_columns(start, width):
    freq_x = frequencies(NX)
    freq_y = lax.dynamic_slice_in_dim(frequencies(NY), start, width)
    freq_z = frequencies(NZ)
    freq_y = jnp.broadcast_to(freq_y[:, None], (width, NZ)).reshape(-1)
    freq_z = jnp.broadcast_to(freq_z[None], (width, NZ)).reshape(-1)
    squared = freq_x[:, None] ** 2 + freq_y[None] ** 2 + freq_z[None] ** 2
    radius = cell_side * (3.0 / (4.0 * math.pi)) ** (1.0 / 3.0)
    safe_square = jnp.where(squared > 0, squared, 1.0)
    general = 4.0 * math.pi * (1.0 - jnp.cos(jnp.sqrt(safe_square) * radius)) / safe_square
    return jnp.where(squared > 0, general, 2.0 * math.pi * radius * radius)


def split_table(table):
    high = table.astype(ml_dtypes.bfloat16)
    low = (table - high.astype(np.float64)).astype(ml_dtypes.bfloat16)
    return high, low


def angle_tables(sign):
    index = np.arange(96)
    angles = 2.0 * np.pi * (np.outer(index, index) % 96) / 96
    return np.cos(angles), sign * np.sin(angles)


def lane_table(sign):
    cosine, sine = angle_tables(sign)
    table = np.zeros((256, 256))
    table[:96, :96] = cosine
    table[128:224, 128:224] = cosine
    table[:96, 128:224] = sine
    table[128:224, :96] = -sine
    return split_table(table)


def slab_order():
    part = np.array([0] * 8 + [1] * 8 + [0] * 4 + [1] * 4)
    virtual = np.array(list(range(8)) * 2 + list(range(8, 12)) * 2)
    slot = np.array([0, 0, 0, 0, 1, 1, 1, 1, 0, 0, 1, 1])[virtual]
    local = np.array([0, 1, 2, 3, 0, 1, 2, 3, 4, 5, 4, 5])[virtual]
    planes = np.array([[0, 1, 2, 3, 8, 9], [4, 5, 6, 7, 10, 11]])
    places = [
        slot * 192 + part * 96 + 12 * f + planes[half][local] for f in range(PARTS) for half in range(2)
    ]
    return np.concatenate(places)


def row_tables():
    order = slab_order()
    cosine, sine = angle_tables(-1.0)
    single = np.block([[cosine, -sine], [sine, cosine]])
    forward = np.kron(np.eye(2), single)[:, order]
    cosine, sine = angle_tables(1.0)
    single = np.block([[cosine, -sine], [sine, cosine]])
    inverse = np.kron(np.eye(2), single)[order]
    return split_table(forward) + split_table(inverse)


def const_times(value, angle, count):
    re, im = value
    angle %= count
    if angle == 0:
        return value
    if 2 * angle == count:
        return (-re, -im)
    if 4 * angle == count:
        return (-im, re)
    if 4 * angle == 3 * count:
        return (im, -re)
    c = math.cos(2 * math.pi * angle / count)
    s = math.sin(2 * math.pi * angle / count)
    if (8 * angle) % count == 0:
        r = math.sqrt(0.5)
        c = math.copysign(1.0, c)
        s = math.copysign(1.0, s)
        a = re * (c * r)
        b = im * (c * r)
        return (a - b, a + b) if c == s else (a + b, b - a)
    return (re * c - im * s, re * s + im * c)


def add(a, b):
    return (a[0] + b[0], a[1] + b[1])


def sub(a, b):
    return (a[0] - b[0], a[1] - b[1])


def small_dft(x, sign):
    n = len(x)
    if n == 2:
        return [add(x[0], x[1]), sub(x[0], x[1])]
    if n == 3:
        total = add(x[1], x[2])
        diff = sub(x[1], x[2])
        r = sign * math.sqrt(0.75)
        mid = (x[0][0] - 0.5 * total[0], x[0][1] - 0.5 * total[1])
        turn = (-r * diff[1], r * diff[0])
        return [add(x[0], total), add(mid, turn), sub(mid, turn)]
    if n == 4:
        a, b = add(x[0], x[2]), sub(x[0], x[2])
        c, d = add(x[1], x[3]), sub(x[1], x[3])
        d = const_times(d, sign, 4)
        return [add(a, c), add(b, d), sub(a, c), sub(b, d)]
    inner = 4
    outer = n // inner
    out = [None] * n
    columns = []
    for low in range(outer):
        column = small_dft([x[outer * i + low] for i in range(inner)], sign)
        columns.append([const_times(v, sign * low * k, n) for k, v in enumerate(column)])
    for k in range(inner):
        row = small_dft([columns[low][k] for low in range(outer)], sign)
        for j in range(outer):
            out[k + inner * j] = row[j]
    return out


def leading_dft(field, sign):
    def tile(t, carry):
        rows = pl.ds(pl.multiple_of(t * 8, 8), 8)

        def load(y):
            return (field[y, rows, 0:128], field[y, rows, 128:256])

        def save(y, v):
            field[y, rows, 0:128] = v[0]
            field[y, rows, 128:256] = v[1]

        for low in range(8):
            column = small_dft([load(8 * i + low) for i in range(12)], sign)
            for k, v in enumerate(column):
                save(8 * k + low, const_times(v, sign * low * k, 96))
        return carry

    lax.fori_loop(0, 3, tile, 0, unroll=UNROLL)


def second_pass(field, k, rows, sign):
    values = [
        (field[8 * k + low, rows, 0:128], field[8 * k + low, rows, 128:256]) for low in range(8)
    ]
    return small_dft(values, sign)


def whole_dft(source, target, sign):
    leading_dft(source, sign)

    def tile(t, carry):
        rows = pl.ds(pl.multiple_of(t * 8, 8), 8)
        for k in range(12):
            for j, v in enumerate(second_pass(source, k, rows, sign)):
                target[k + 12 * j, rows, 0:128] = v[0]
                target[k + 12 * j, rows, 128:256] = v[1]
        return carry

    lax.fori_loop(0, 3, tile, 0, unroll=UNROLL)


def lanes():
    return lax.broadcasted_iota(jnp.int32, (8, 128), 1)


def unpack(wide):
    lane = lanes()
    out = []
    for q in range(3):
        a, b, c = (wide[:, 128 * (3 * q + i) : 128 * (3 * q + i + 1)] for i in range(3))
        out.append(a)
        out.append(jnp.where(lane < 32, pltpu.roll(a, 32, 1), pltpu.roll(b, 32, 1)))
        out.append(jnp.where(lane < 64, pltpu.roll(b, 64, 1), pltpu.roll(c, 64, 1)))
        out.append(pltpu.roll(c, 96, 1))
    return out


def pack(tiles):
    lane = lanes()
    out = []
    for q in range(3):
        a, b, c, d = tiles[4 * q : 4 * q + 4]
        b = pltpu.roll(b, 96, 1)
        c = pltpu.roll(c, 64, 1)
        d = pltpu.roll(d, 32, 1)
        out.append(jnp.where(lane < 96, a, b))
        out.append(jnp.where(lane < 64, b, c))
        out.append(jnp.where(lane < 32, c, d))
    return jnp.concatenate(out, axis=1)


def flip(x):
    return pltpu.roll(x, 4, 0)


def top(x):
    return lax.broadcasted_iota(jnp.int32, x.shape, 0) < 4


def split_dot(x, high, low):
    x_high = x.astype(jnp.bfloat16)
    x_low = (x - x_high.astype(jnp.float32)).astype(jnp.bfloat16)
    dot = functools.partial(jnp.dot, preferred_element_type=jnp.float32)
    return dot(x_high, high) + (dot(x_high, low) + dot(x_low, high))


def dot_split(high, low, x):
    x_high = x.astype(jnp.bfloat16)
    x_low = (x - x_high.astype(jnp.float32)).astype(jnp.bfloat16)
    dot = functools.partial(jnp.dot, preferred_element_type=jnp.float32)
    return dot(high, x_high) + (dot(low, x_high) + dot(high, x_low))


def row_index(x):
    return lax.broadcasted_iota(jnp.int32, x.shape, 0)


def combine(a0, a1, b0, b1):
    upper = top(a0)
    row = row_index(b0)
    rest = jnp.where(
        row < 2,
        b0,
        jnp.where(
            row < 4,
            pltpu.roll(b1, 2, 0),
            jnp.where(row < 6, pltpu.roll(b0, 2, 0), pltpu.roll(b1, 4, 0)),
        ),
    )
    return jnp.where(upper, a0, flip(a1)), jnp.where(upper, flip(a0), a1), rest


def split(t0, t1, t2):
    upper = top(t0)
    low = row_index(t2) < 2
    back = pltpu.roll(t2, 6, 0)
    return (
        jnp.where(upper, t0, flip(t1)),
        jnp.where(upper, flip(t0), t1),
        jnp.where(low, t2, back),
        jnp.where(low, back, flip(t2)),
    )


def list_load(ref, start):
    x = ref[pl.ds(pl.multiple_of(start, 8), 72), :]
    return jnp.concatenate([x[8 * i : 8 * i + 8] for i in range(9)], axis=1)


def list_save(ref, start, x):
    for i in range(9):
        ref[pl.ds(pl.multiple_of(start + 8 * i, 8), 8), :] = x[:, 128 * i : 128 * i + 128]


def second_start(g):
    return 8 * (72 + 9 * lax.rem(g, 4))


def half_load(ref, g):
    b = list_load(ref, second_start(g))
    return list_load(ref, 72 * g), jnp.where(g >= 4, flip(b), b)


def half_save(ref, g, a, b):
    list_save(ref, 72 * g, a)
    old = list_load(ref, second_start(g))
    upper = top(b)
    b = jnp.where(upper, b, flip(b))
    b = jnp.where(g < 4, jnp.where(upper, b, old), jnp.where(upper, old, b))
    list_save(ref, second_start(g), b)


def block_columns(g):
    return pl.ds(pl.multiple_of(g * BLOCK, 128), BLOCK)


def slab_rows(ref, g):
    cols = block_columns(g)
    rest = jnp.concatenate([ref[0, 8:12, cols], ref[1, 8:12, cols]], axis=0)
    return ref[0, 0:8, cols], ref[1, 0:8, cols], rest


def orbital_rows(ref, g):
    cols = block_columns(g)
    return ref[0:8, cols], ref[8:16, cols], ref[16:24, cols]


def halves_kernel(place, orbital, keep, send):
    first = place[2] == 0

    def block(g, carry):
        a0, a1, b0, b1 = split(*slab_rows(orbital, g))
        half_save(keep, g, jnp.where(first, a0, a1), jnp.where(first, b0, b1))
        half_save(send, g, jnp.where(first, a1, a0), jnp.where(first, b1, b0))
        return carry

    lax.fori_loop(0, PARTS, block, 0, unroll=UNROLL)
    for ref in (keep, send):
        ref[TILES:LIST, :] = jnp.zeros((LIST - TILES, 128), jnp.float32)


def applied_kernel(place, near, got, far, out):
    first = place[2] == 0

    def block(g, carry):
        cols = block_columns(g)
        a0, b0 = half_load(near, g)
        a1, b1 = half_load(got, g)
        a0, b0 = a0 + a1, b0 + b1
        a1, b1 = half_load(far, g)
        t0, t1, t2 = combine(
            jnp.where(first, a0, a1),
            jnp.where(first, a1, a0),
            jnp.where(first, b0, b1),
            jnp.where(first, b1, b0),
        )
        for part, rows, rest in ((0, t0, t2[0:4]), (1, t1, t2[4:8])):
            for x in range(12):
                row = rows[x : x + 1] if x < 8 else rest[x - 8 : x - 7]
                out[x, part : part + 1, cols] = row
        return carry

    lax.fori_loop(0, PARTS, block, 0, unroll=UNROLL)


def served_rows(ref, g):
    a, b = half_load(ref, g)
    return combine(a, a, b, b)


def forward_kernel(
    place, served, keep, recv, keep_other, recv_other, table, out, mine, other, line, field, spectrum
):
    first = place[2] == 0

    def block(g, carry):
        s0, s1, s2 = served_rows(served, g)
        parts = []
        rests = []
        cols = block_columns(g)
        for own, far, ref in ((keep, recv, mine), (keep_other, recv_other, other)):
            (a0, b0), (a1, b1) = half_load(own, g), half_load(far, g)
            re, im, rest = combine(
                jnp.where(first, a0, a1),
                jnp.where(first, a1, a0),
                jnp.where(first, b0, b1),
                jnp.where(first, b1, b0),
            )
            for r, rows in enumerate((re, im, rest)):
                ref[8 * r : 8 * r + 8, cols] = rows
            parts.append((s0 * re + s1 * im, s0 * im - s1 * re))
            same = s2 * rest
            cross = s2 * flip(rest)
            rests.append((same + flip(same), cross - flip(cross)))
        upper = top(s2)
        parts.append(
            (jnp.where(upper, rests[0][0], rests[1][0]), jnp.where(upper, rests[0][1], -rests[1][1]))
        )
        for t, (re, im) in enumerate(parts):
            for y, (a, b) in enumerate(zip(unpack(re), unpack(im))):
                line[24 * y + 8 * t : 24 * y + 8 * t + 8, 0:128] = a
                line[24 * y + 8 * t : 24 * y + 8 * t + 8, 128:256] = b
        result = split_dot(line[...], table[0:256], table[256:512])
        field[pl.ds(g * 12, 12)] = result.reshape(12, 24, 256)
        return carry

    lax.fori_loop(0, PARTS, block, 0, unroll=UNROLL)
    whole_dft(field, spectrum, -1)

    def send(g, carry):
        packed = []
        for t in range(3):
            rows = slice(8 * t, 8 * t + 8)
            packed.append(
                tuple(
                    pack([spectrum[g * 12 + y, rows, c : c + 128] for y in range(12)])
                    for c in (0, 128)
                )
            )
        re, im = packed[2]
        upper = top(re)
        for p, rest in enumerate(
            (jnp.where(upper, re, flip(im)), jnp.where(upper, flip(re), im))
        ):
            out[g, p, 0:8, :] = packed[p][0]
            out[g, p, 8:16, :] = packed[p][1]
            out[g, p, 16:24, :] = rest
        return carry

    lax.fori_loop(0, PARTS, send, 0, unroll=UNROLL)


def column_kernel(blocks, coulomb, tables, out):
    width = BLOCK // 3
    for i in range(3):
        cols = slice(width * i, width * i + width)
        x = blocks[:, :, cols].reshape(16 * ROWS, width)
        x = dot_split(tables[0:384], tables[384:768], x)
        k = coulomb[:, cols]
        x = jnp.concatenate([x[96 * j : 96 * j + 96] * k for j in range(4)], axis=0)
        x = dot_split(tables[768:1152], tables[1152:1536], x)
        out[:, :, cols] = x.reshape(16, ROWS, width)


def backward_kernel(
    place, blocks, served, mine, other, table, own_near, own_far, away_near, away_far, terms,
    line, field, spectrum, total,
):
    first = place[2] == 0

    def receive(g, carry):
        rests = [blocks[g, p, 16:24, :] for p in range(2)]
        upper = top(rests[0])
        parts = [(blocks[g, p, 0:8, :], blocks[g, p, 8:16, :]) for p in range(2)]
        parts.append(
            (
                jnp.where(upper, rests[0], flip(rests[1])),
                jnp.where(upper, flip(rests[0]), rests[1]),
            )
        )
        for t, (re, im) in enumerate(parts):
            rows = slice(8 * t, 8 * t + 8)
            for y, (a, b) in enumerate(zip(unpack(re), unpack(im))):
                spectrum[g * 12 + y, rows, 0:128] = a
                spectrum[g * 12 + y, rows, 128:256] = b
        return carry

    lax.fori_loop(0, PARTS, receive, 0, unroll=UNROLL)
    whole_dft(spectrum, field, 1)

    def block(g, carry):
        x = field[pl.ds(g * 12, 12)].reshape(288, 256)
        line[...] = split_dot(x, table[0:256], table[256:512])
        packed = []
        for t in range(3):
            packed.append(
                tuple(
                    pack([line[24 * y + 8 * t : 24 * y + 8 * t + 8, c : c + 128] for y in range(12)])
                    for c in (0, 128)
                )
            )
        re, im = packed[2]
        upper = top(re)
        rests = (jnp.where(upper, re, flip(im)), jnp.where(upper, flip(re), im))
        s0, s1, s2 = served_rows(served, g)
        sums = None
        for p, (ref, near, far) in enumerate(
            ((mine, own_near, own_far), (other, away_near, away_far))
        ):
            vr, vi = packed[p]
            v2 = rests[p]
            same = s2 * v2
            cross = s2 * flip(v2)
            a0, a1, b0, b1 = split(
                s0 * vr - s1 * vi,
                s0 * vi + s1 * vr,
                jnp.where(upper, same - flip(same), cross + flip(cross)),
            )
            half_save(near, g, jnp.where(first, a0, a1), jnp.where(first, b0, b1))
            half_save(far, g, jnp.where(first, a1, a0), jnp.where(first, b1, b0))
            ore, oim, rest = orbital_rows(ref, g)
            same = v2 * rest
            cross = v2 * flip(rest)
            turned = flip(cross)
            both = (
                vr * ore + vi * oim,
                vr * oim - vi * ore,
                jnp.where(upper, same + flip(same), turned - cross),
            )
            sums = both if sums is None else tuple(a + b for a, b in zip(sums, both))
        a0, a1, b0, b1 = split(*sums)
        half_save(total, g, a0 + a1, b0 + b1)
        return carry

    lax.fori_loop(0, PARTS, block, 0, unroll=UNROLL)
    lane = lanes()

    def tile(l):
        return total[8 * l : 8 * l + 8, :]

    def turn(x):
        return pltpu.roll(x, 64, 1)

    for g in range(4):
        middle = 9 * g + 4
        for odd in range(2):
            begin = 9 * g + 5 * odd
            tiles = [tile(begin + i) for i in range(4)] + [tile(begin + 36 + i) for i in range(4)]
            a, b = tile(middle), tile(middle + 36)
            a, b = (turn(a), b) if odd else (a, turn(b))
            tiles.append(jnp.where(lane < 64, a, b))
            tiles += [tile(72 + begin + i) for i in range(4)]
            a = tile(72 + middle)
            tiles.append(turn(a) if odd else a)
            for i, x in enumerate(tiles):
                start = (2 * g + odd) * CHUNK + 8 * i
                terms[start : start + 8, :] = x


def finish_kernel(place, blocks, *pieces):
    lane = lanes()
    second_core = place[0] == 1
    odd = place[1] == 1
    second_half = place[2] == 1
    tiles = []
    for i in range(14):
        x = [blocks[CHUNK * q + 8 * i : CHUNK * q + 8 * i + 8, :] for q in range(8)]
        while len(x) > 1:
            x = [x[2 * j] + x[2 * j + 1] for j in range(len(x) // 2)]
        tiles.append(x[0])

    def widen(f, h):
        s = [pltpu.roll(x, 64, 1) for x in f]
        wide = [
            jnp.where(odd, jnp.where(lane < 64, a, b), c)
            for a, b, c in zip([h] + s, s + [s[3]], f + [h])
        ]
        s = [pltpu.roll(x, 96, 1) for x in wide[2:]]
        second = [jnp.where(lane < 96, s[0], s[1]), jnp.where(lane < 96, s[1], s[2]), s[2]]
        return wide[:3], second

    left = widen(tiles[0:4], tiles[8])
    right = widen(tiles[4:8], pltpu.roll(tiles[8], 64, 1))
    rest = widen(tiles[9:13], tiles[13])
    for piece, out in enumerate(pieces):
        half = second_half if piece < 2 else jnp.logical_not(second_half)
        core = second_core if piece % 2 == 0 else jnp.logical_not(second_core)
        for i in range(3):
            x = [jnp.where(core, y[1][i], y[0][i]) for y in (left, right, rest)]
            a = jnp.where(half, x[1], x[0])
            b = jnp.where(half, flip(x[2]), x[2])
            width = 128 if i < 2 else 32
            cols = slice(128 * i, 128 * i + width)
            out[0:8, cols] = a[:, :width]
            out[8:12, cols] = b[0:4, :width]


def serving_kernel(place, p00, p01, p10, p11, out):
    second_core = place[0] == 1
    second_half = place[2] == 1
    x = [[p00[...], p01[...]], [p10[...], p11[...]]]
    for member in range(2):
        swap = second_core if member == 0 else jnp.logical_not(second_core)
        near, far = (jnp.where(swap, x[i][1], x[i][0]) for i in range(2))
        h0 = jnp.where(second_half, far, near)
        h1 = jnp.where(second_half, near, far)
        for part in range(2):
            for i in range(12):
                source = h0 if i in (0, 1, 2, 3, 8, 9) else h1
                j = i % 4 + 4 * part if i < 8 else 8 + i % 2 + 2 * part
                out[member, i, part : part + 1, :] = source[j : j + 1]


def f32(*shape):
    return jax.ShapeDtypeStruct(shape, jnp.float32)


def shards(orbitals, serve_order):
    rank_fft = lax.axis_index("fft")
    rank_band = lax.axis_index("band")
    core = rank_band % 2
    line = rank_band // 2 % 8
    half = rank_band // 16
    place = jnp.stack([core, line % 2, half]).astype(jnp.int32)
    z_groups = [[y * 16 + 2 * z + c for z in range(8)] for y in range(2) for c in range(2)]
    plane_groups = [
        [(y * 16 + b) * PARTS + f for f in range(PARTS) for y in range(2)] for b in range(16)
    ]
    scale = -mixing / (NX * NY * NZ)

    coulomb = kernel_columns(rank_fft * 12, 12) * scale
    params = pltpu.CompilerParams(vmem_limit_bytes=VMEM)
    scalars = pl.BlockSpec(memory_space=pltpu.SMEM)
    whole = pl.BlockSpec(memory_space=pltpu.VMEM)

    def call(kernel, shapes, inputs, scratch=()):
        return pl.pallas_call(
            kernel,
            out_shape=shapes,
            in_specs=[scalars] + [whole] * len(inputs),
            out_specs=jax.tree.map(lambda _: whole, shapes),
            scratch_shapes=list(scratch),
            compiler_params=params,
        )(place, *inputs)

    def swap(x, bits):
        return lax.ppermute(x, "band", [(i, i ^ bits) for i in range(32)])

    def line_exchange(blocks):
        return lax.all_to_all(blocks, "band", 0, 0, axis_index_groups=z_groups, tiled=True)

    def plane_exchange(blocks):
        return lax.all_to_all(
            blocks, ("band", "fft"), 0, 0, axis_index_groups=plane_groups, tiled=True
        )

    lists = f32(LIST, 128)
    keep, send = call(halves_kernel, (lists, lists), (orbitals.reshape(2, 12, PLANE),))
    upper, lower = swap(send[:576], 16), swap(send[576:], 16)
    lower, coulomb = lax.optimization_barrier((lower, coulomb))
    keep_other = swap(keep, 1)
    recv = jnp.concatenate([upper, lower])
    recv_other = jnp.concatenate([swap(upper, 1), swap(lower, 1)])
    serving = serve_order[core]
    near = serving // 16 == half
    same = serving % 2 == core
    candidate = jnp.where(
        same, jnp.where(near, keep, recv), jnp.where(near, keep_other, recv_other)
    )
    blocks = line_exchange(candidate.reshape(8, CHUNK, 128))
    block = lax.dynamic_index_in_dim(blocks, serving // 2 % 8, 0, keepdims=True)
    served = line_exchange(jnp.broadcast_to(block, blocks.shape)).reshape(LIST, 128)

    scratch = [
        pltpu.VMEM((288, 256), jnp.float32),
        pltpu.VMEM((NY, ROWS, 256), jnp.float32),
        pltpu.VMEM((NY, ROWS, 256), jnp.float32),
    ]
    table = jnp.asarray(np.concatenate(lane_table(-1.0)))
    rows = f32(ROWS, PLANE)
    blocks, mine, other = call(
        forward_kernel,
        (f32(PARTS, 2, ROWS, BLOCK), rows, rows),
        (served, keep, recv, keep_other, recv_other, table),
        scratch,
    )
    blocks = plane_exchange(blocks.reshape(16, ROWS, BLOCK))
    tables = jnp.asarray(np.concatenate(row_tables()))
    blocks = pl.pallas_call(
        column_kernel,
        out_shape=f32(16, ROWS, BLOCK),
        in_specs=[whole] * 3,
        out_specs=whole,
        compiler_params=params,
    )(blocks, coulomb, tables)
    blocks = plane_exchange(blocks).reshape(PARTS, 2, ROWS, BLOCK)
    table = jnp.asarray(np.concatenate(lane_table(1.0)))
    short = f32(TILES, 128)
    own_near, own_far, away_near, away_far, terms = call(
        backward_kernel,
        (short, short, short, short, lists),
        (blocks, served, mine, other, table),
        scratch + [pltpu.VMEM((TILES, 128), jnp.float32)],
    )
    far = swap(own_far + swap(away_far, 1), 16)
    got = swap(away_near, 1)
    applied = call(applied_kernel, f32(12, 2, PLANE), (own_near, got, far))
    blocks = line_exchange(terms.reshape(8, CHUNK, 128)).reshape(LIST, 128)
    blocks, applied = lax.optimization_barrier((blocks, applied))
    small = f32(12, HALF)
    pieces = call(finish_kernel, (small,) * 4, (blocks,))
    pieces = [pieces[0], swap(pieces[1], 1), swap(pieces[2], 16), swap(pieces[3], 17)]
    serving_exchange = call(serving_kernel, f32(SERVE, 12, 2, HALF), pieces)
    return (applied.transpose(1, 0, 2)[None], serving_exchange.transpose(0, 2, 1, 3))


def solution(mesh):
    return jax.shard_map(
        shards,
        mesh=mesh,
        in_specs=(P("band", None, "fft", None), P()),
        out_specs=(P("band", None, "fft", None), P(None, None, "fft", "band")),
        check_vma=False,
    )
```

```python
import functools
import math

import jax
import jax.numpy as jnp
import ml_dtypes
import numpy as np
from jax import lax
from jax.experimental import pallas as pl
from jax.experimental.pallas import tpu as pltpu
from jax.sharding import PartitionSpec as P

NX = 96
NY = 96
NZ = 96
SERVE = 2
CHIPS = 16
PARTS = 8
ROWS = 24
PLANE = NY * NZ
BLOCK = PLANE // PARTS
CHUNK = 112
LIST = 8 * CHUNK
TILES = 108 * 8
HALF = PLANE // CHIPS // 2
UNROLL = True
VMEM = 48 * 1024 * 1024

cell_side = 41.04
mixing = 0.25


def frequencies(count):
    signed = (jnp.arange(count, dtype=jnp.int32) + count // 2) % count - count // 2
    return signed.astype(jnp.float32) * (2.0 * math.pi / cell_side)


def kernel_columns(start, width):
    freq_x = frequencies(NX)
    freq_y = lax.dynamic_slice_in_dim(frequencies(NY), start, width)
    freq_z = frequencies(NZ)
    freq_y = jnp.broadcast_to(freq_y[:, None], (width, NZ)).reshape(-1)
    freq_z = jnp.broadcast_to(freq_z[None], (width, NZ)).reshape(-1)
    squared = freq_x[:, None] ** 2 + freq_y[None] ** 2 + freq_z[None] ** 2
    radius = cell_side * (3.0 / (4.0 * math.pi)) ** (1.0 / 3.0)
    safe_square = jnp.where(squared > 0, squared, 1.0)
    general = 4.0 * math.pi * (1.0 - jnp.cos(jnp.sqrt(safe_square) * radius)) / safe_square
    return jnp.where(squared > 0, general, 2.0 * math.pi * radius * radius)


def split_table(table):
    high = table.astype(ml_dtypes.bfloat16)
    low = (table - high.astype(np.float64)).astype(ml_dtypes.bfloat16)
    return high, low


def angle_tables(sign):
    index = np.arange(96)
    angles = 2.0 * np.pi * (np.outer(index, index) % 96) / 96
    return np.cos(angles), sign * np.sin(angles)


def lane_table(sign):
    cosine, sine = angle_tables(sign)
    table = np.zeros((256, 256))
    table[:96, :96] = cosine
    table[128:224, 128:224] = cosine
    table[:96, 128:224] = sine
    table[128:224, :96] = -sine
    return split_table(table)


def slab_order():
    part = np.array([0] * 8 + [1] * 8 + [0] * 4 + [1] * 4)
    virtual = np.array(list(range(8)) * 2 + list(range(8, 12)) * 2)
    slot = np.array([0, 0, 0, 0, 1, 1, 1, 1, 0, 0, 1, 1])[virtual]
    local = np.array([0, 1, 2, 3, 0, 1, 2, 3, 4, 5, 4, 5])[virtual]
    planes = np.array([[0, 1, 2, 3, 8, 9], [4, 5, 6, 7, 10, 11]])
    places = [
        slot * 192 + part * 96 + 12 * f + planes[half][local] for f in range(PARTS) for half in range(2)
    ]
    return np.concatenate(places)


def row_tables():
    order = slab_order()
    cosine, sine = angle_tables(-1.0)
    single = np.block([[cosine, -sine], [sine, cosine]])
    forward = np.kron(np.eye(2), single)[:, order]
    cosine, sine = angle_tables(1.0)
    single = np.block([[cosine, -sine], [sine, cosine]])
    inverse = np.kron(np.eye(2), single)[order]
    return split_table(forward) + split_table(inverse)


def const_times(value, angle, count):
    re, im = value
    angle %= count
    if angle == 0:
        return value
    if 2 * angle == count:
        return (-re, -im)
    if 4 * angle == count:
        return (-im, re)
    if 4 * angle == 3 * count:
        return (im, -re)
    c = math.cos(2 * math.pi * angle / count)
    s = math.sin(2 * math.pi * angle / count)
    if (8 * angle) % count == 0:
        r = math.sqrt(0.5)
        c = math.copysign(1.0, c)
        s = math.copysign(1.0, s)
        a = re * (c * r)
        b = im * (c * r)
        return (a - b, a + b) if c == s else (a + b, b - a)
    return (re * c - im * s, re * s + im * c)


def add(a, b):
    return (a[0] + b[0], a[1] + b[1])


def sub(a, b):
    return (a[0] - b[0], a[1] - b[1])


def small_dft(x, sign):
    n = len(x)
    if n == 2:
        return [add(x[0], x[1]), sub(x[0], x[1])]
    if n == 3:
        total = add(x[1], x[2])
        diff = sub(x[1], x[2])
        r = sign * math.sqrt(0.75)
        mid = (x[0][0] - 0.5 * total[0], x[0][1] - 0.5 * total[1])
        turn = (-r * diff[1], r * diff[0])
        return [add(x[0], total), add(mid, turn), sub(mid, turn)]
    if n == 4:
        a, b = add(x[0], x[2]), sub(x[0], x[2])
        c, d = add(x[1], x[3]), sub(x[1], x[3])
        d = const_times(d, sign, 4)
        return [add(a, c), add(b, d), sub(a, c), sub(b, d)]
    inner = 4
    outer = n // inner
    out = [None] * n
    columns = []
    for low in range(outer):
        column = small_dft([x[outer * i + low] for i in range(inner)], sign)
        columns.append([const_times(v, sign * low * k, n) for k, v in enumerate(column)])
    for k in range(inner):
        row = small_dft([columns[low][k] for low in range(outer)], sign)
        for j in range(outer):
            out[k + inner * j] = row[j]
    return out


def leading_dft(field, sign):
    def tile(t, carry):
        rows = pl.ds(pl.multiple_of(t * 8, 8), 8)

        def load(y):
            return (field[y, rows, 0:128], field[y, rows, 128:256])

        def save(y, v):
            field[y, rows, 0:128] = v[0]
            field[y, rows, 128:256] = v[1]

        for low in range(8):
            column = small_dft([load(8 * i + low) for i in range(12)], sign)
            for k, v in enumerate(column):
                save(8 * k + low, const_times(v, sign * low * k, 96))
        return carry

    lax.fori_loop(0, 3, tile, 0, unroll=UNROLL)


def second_pass(field, k, rows, sign):
    values = [
        (field[8 * k + low, rows, 0:128], field[8 * k + low, rows, 128:256]) for low in range(8)
    ]
    return small_dft(values, sign)


def whole_dft(source, target, sign):
    leading_dft(source, sign)

    def tile(t, carry):
        rows = pl.ds(pl.multiple_of(t * 8, 8), 8)
        for k in range(12):
            for j, v in enumerate(second_pass(source, k, rows, sign)):
                target[k + 12 * j, rows, 0:128] = v[0]
                target[k + 12 * j, rows, 128:256] = v[1]
        return carry

    lax.fori_loop(0, 3, tile, 0, unroll=UNROLL)


def lanes():
    return lax.broadcasted_iota(jnp.int32, (8, 128), 1)


def unpack(wide):
    lane = lanes()
    out = []
    for q in range(3):
        a, b, c = (wide[:, 128 * (3 * q + i) : 128 * (3 * q + i + 1)] for i in range(3))
        out.append(a)
        out.append(jnp.where(lane < 32, pltpu.roll(a, 32, 1), pltpu.roll(b, 32, 1)))
        out.append(jnp.where(lane < 64, pltpu.roll(b, 64, 1), pltpu.roll(c, 64, 1)))
        out.append(pltpu.roll(c, 96, 1))
    return out


def pack(tiles):
    lane = lanes()
    out = []
    for q in range(3):
        a, b, c, d = tiles[4 * q : 4 * q + 4]
        b = pltpu.roll(b, 96, 1)
        c = pltpu.roll(c, 64, 1)
        d = pltpu.roll(d, 32, 1)
        out.append(jnp.where(lane < 96, a, b))
        out.append(jnp.where(lane < 64, b, c))
        out.append(jnp.where(lane < 32, c, d))
    return jnp.concatenate(out, axis=1)


def flip(x):
    return pltpu.roll(x, 4, 0)


def top(x):
    return lax.broadcasted_iota(jnp.int32, x.shape, 0) < 4


def split_dot(x, high, low):
    x_high = x.astype(jnp.bfloat16)
    x_low = (x - x_high.astype(jnp.float32)).astype(jnp.bfloat16)
    dot = functools.partial(jnp.dot, preferred_element_type=jnp.float32)
    return dot(x_high, high) + (dot(x_high, low) + dot(x_low, high))


def dot_split(high, low, x):
    x_high = x.astype(jnp.bfloat16)
    x_low = (x - x_high.astype(jnp.float32)).astype(jnp.bfloat16)
    dot = functools.partial(jnp.dot, preferred_element_type=jnp.float32)
    return dot(high, x_high) + (dot(low, x_high) + dot(high, x_low))


def row_index(x):
    return lax.broadcasted_iota(jnp.int32, x.shape, 0)


def combine(a0, a1, b0, b1):
    upper = top(a0)
    row = row_index(b0)
    rest = jnp.where(
        row < 2,
        b0,
        jnp.where(
            row < 4,
            pltpu.roll(b1, 2, 0),
            jnp.where(row < 6, pltpu.roll(b0, 2, 0), pltpu.roll(b1, 4, 0)),
        ),
    )
    return jnp.where(upper, a0, flip(a1)), jnp.where(upper, flip(a0), a1), rest


def split(t0, t1, t2):
    upper = top(t0)
    low = row_index(t2) < 2
    back = pltpu.roll(t2, 6, 0)
    return (
        jnp.where(upper, t0, flip(t1)),
        jnp.where(upper, flip(t0), t1),
        jnp.where(low, t2, back),
        jnp.where(low, back, flip(t2)),
    )


def list_load(ref, start):
    x = ref[pl.ds(pl.multiple_of(start, 8), 72), :]
    return jnp.concatenate([x[8 * i : 8 * i + 8] for i in range(9)], axis=1)


def list_save(ref, start, x):
    for i in range(9):
        ref[pl.ds(pl.multiple_of(start + 8 * i, 8), 8), :] = x[:, 128 * i : 128 * i + 128]


def second_start(g):
    return 8 * (72 + 9 * lax.rem(g, 4))


def half_load(ref, g):
    b = list_load(ref, second_start(g))
    return list_load(ref, 72 * g), jnp.where(g >= 4, flip(b), b)


def half_save(ref, g, a, b):
    list_save(ref, 72 * g, a)
    old = list_load(ref, second_start(g))
    upper = top(b)
    b = jnp.where(upper, b, flip(b))
    b = jnp.where(g < 4, jnp.where(upper, b, old), jnp.where(upper, old, b))
    list_save(ref, second_start(g), b)


def block_columns(g):
    return pl.ds(pl.multiple_of(g * BLOCK, 128), BLOCK)


def slab_rows(ref, g):
    cols = block_columns(g)
    rest = jnp.concatenate([ref[0, 8:12, cols], ref[1, 8:12, cols]], axis=0)
    return ref[0, 0:8, cols], ref[1, 0:8, cols], rest


def orbital_rows(ref, g):
    cols = block_columns(g)
    return ref[0:8, cols], ref[8:16, cols], ref[16:24, cols]


def halves_kernel(place, orbital, keep, send):
    first = place[2] == 0

    def block(g, carry):
        a0, a1, b0, b1 = split(*slab_rows(orbital, g))
        half_save(keep, g, jnp.where(first, a0, a1), jnp.where(first, b0, b1))
        half_save(send, g, jnp.where(first, a1, a0), jnp.where(first, b1, b0))
        return carry

    lax.fori_loop(0, PARTS, block, 0, unroll=UNROLL)
    for ref in (keep, send):
        ref[TILES:LIST, :] = jnp.zeros((LIST - TILES, 128), jnp.float32)


def applied_kernel(place, near, got, far, out):
    first = place[2] == 0

    def block(g, carry):
        cols = block_columns(g)
        a0, b0 = half_load(near, g)
        a1, b1 = half_load(got, g)
        a0, b0 = a0 + a1, b0 + b1
        a1, b1 = half_load(far, g)
        t0, t1, t2 = combine(
            jnp.where(first, a0, a1),
            jnp.where(first, a1, a0),
            jnp.where(first, b0, b1),
            jnp.where(first, b1, b0),
        )
        for part, rows, rest in ((0, t0, t2[0:4]), (1, t1, t2[4:8])):
            for x in range(12):
                row = rows[x : x + 1] if x < 8 else rest[x - 8 : x - 7]
                out[x, part : part + 1, cols] = row
        return carry

    lax.fori_loop(0, PARTS, block, 0, unroll=UNROLL)


def served_rows(ref, g):
    a, b = half_load(ref, g)
    return combine(a, a, b, b)


def forward_kernel(
    place, served, keep, recv, keep_other, recv_other, table, out, mine, other, line, field, spectrum
):
    first = place[2] == 0

    def block(g, carry):
        s0, s1, s2 = served_rows(served, g)
        parts = []
        rests = []
        cols = block_columns(g)
        for own, far, ref in ((keep, recv, mine), (keep_other, recv_other, other)):
            (a0, b0), (a1, b1) = half_load(own, g), half_load(far, g)
            re, im, rest = combine(
                jnp.where(first, a0, a1),
                jnp.where(first, a1, a0),
                jnp.where(first, b0, b1),
                jnp.where(first, b1, b0),
            )
            for r, rows in enumerate((re, im, rest)):
                ref[8 * r : 8 * r + 8, cols] = rows
            parts.append((s0 * re + s1 * im, s0 * im - s1 * re))
            same = s2 * rest
            cross = s2 * flip(rest)
            rests.append((same + flip(same), cross - flip(cross)))
        upper = top(s2)
        parts.append(
            (jnp.where(upper, rests[0][0], rests[1][0]), jnp.where(upper, rests[0][1], -rests[1][1]))
        )
        for t, (re, im) in enumerate(parts):
            for y, (a, b) in enumerate(zip(unpack(re), unpack(im))):
                line[24 * y + 8 * t : 24 * y + 8 * t + 8, 0:128] = a
                line[24 * y + 8 * t : 24 * y + 8 * t + 8, 128:256] = b
        result = split_dot(line[...], table[0:256], table[256:512])
        field[pl.ds(g * 12, 12)] = result.reshape(12, 24, 256)
        return carry

    lax.fori_loop(0, PARTS, block, 0, unroll=UNROLL)
    whole_dft(field, spectrum, -1)

    def send(g, carry):
        packed = []
        for t in range(3):
            rows = slice(8 * t, 8 * t + 8)
            packed.append(
                tuple(
                    pack([spectrum[g * 12 + y, rows, c : c + 128] for y in range(12)])
                    for c in (0, 128)
                )
            )
        re, im = packed[2]
        upper = top(re)
        for p, rest in enumerate(
            (jnp.where(upper, re, flip(im)), jnp.where(upper, flip(re), im))
        ):
            out[g, p, 0:8, :] = packed[p][0]
            out[g, p, 8:16, :] = packed[p][1]
            out[g, p, 16:24, :] = rest
        return carry

    lax.fori_loop(0, PARTS, send, 0, unroll=UNROLL)


def column_kernel(blocks, coulomb, tables, out):
    width = BLOCK // 3
    for i in range(3):
        cols = slice(width * i, width * i + width)
        x = blocks[:, :, cols].reshape(16 * ROWS, width)
        x = dot_split(tables[0:384], tables[384:768], x)
        k = coulomb[:, cols]
        x = jnp.concatenate([x[96 * j : 96 * j + 96] * k for j in range(4)], axis=0)
        x = dot_split(tables[768:1152], tables[1152:1536], x)
        out[:, :, cols] = x.reshape(16, ROWS, width)


def backward_kernel(
    place, blocks, served, mine, other, table, own_near, own_far, away_near, away_far, terms,
    line, field, spectrum, total,
):
    first = place[2] == 0

    def receive(g, carry):
        rests = [blocks[g, p, 16:24, :] for p in range(2)]
        upper = top(rests[0])
        parts = [(blocks[g, p, 0:8, :], blocks[g, p, 8:16, :]) for p in range(2)]
        parts.append(
            (
                jnp.where(upper, rests[0], flip(rests[1])),
                jnp.where(upper, flip(rests[0]), rests[1]),
            )
        )
        for t, (re, im) in enumerate(parts):
            rows = slice(8 * t, 8 * t + 8)
            for y, (a, b) in enumerate(zip(unpack(re), unpack(im))):
                spectrum[g * 12 + y, rows, 0:128] = a
                spectrum[g * 12 + y, rows, 128:256] = b
        return carry

    lax.fori_loop(0, PARTS, receive, 0, unroll=UNROLL)
    whole_dft(spectrum, field, 1)

    def block(g, carry):
        x = field[pl.ds(g * 12, 12)].reshape(288, 256)
        line[...] = split_dot(x, table[0:256], table[256:512])
        packed = []
        for t in range(3):
            packed.append(
                tuple(
                    pack([line[24 * y + 8 * t : 24 * y + 8 * t + 8, c : c + 128] for y in range(12)])
                    for c in (0, 128)
                )
            )
        re, im = packed[2]
        upper = top(re)
        rests = (jnp.where(upper, re, flip(im)), jnp.where(upper, flip(re), im))
        s0, s1, s2 = served_rows(served, g)
        sums = None
        for p, (ref, near, far) in enumerate(
            ((mine, own_near, own_far), (other, away_near, away_far))
        ):
            vr, vi = packed[p]
            v2 = rests[p]
            same = s2 * v2
            cross = s2 * flip(v2)
            a0, a1, b0, b1 = split(
                s0 * vr - s1 * vi,
                s0 * vi + s1 * vr,
                jnp.where(upper, same - flip(same), cross + flip(cross)),
            )
            half_save(near, g, jnp.where(first, a0, a1), jnp.where(first, b0, b1))
            half_save(far, g, jnp.where(first, a1, a0), jnp.where(first, b1, b0))
            ore, oim, rest = orbital_rows(ref, g)
            same = v2 * rest
            cross = v2 * flip(rest)
            turned = flip(cross)
            both = (
                vr * ore + vi * oim,
                vr * oim - vi * ore,
                jnp.where(upper, same + flip(same), turned - cross),
            )
            sums = both if sums is None else tuple(a + b for a, b in zip(sums, both))
        a0, a1, b0, b1 = split(*sums)
        half_save(total, g, a0 + a1, b0 + b1)
        return carry

    lax.fori_loop(0, PARTS, block, 0, unroll=UNROLL)
    lane = lanes()

    def tile(l):
        return total[8 * l : 8 * l + 8, :]

    def turn(x):
        return pltpu.roll(x, 64, 1)

    for g in range(4):
        middle = 9 * g + 4
        for odd in range(2):
            begin = 9 * g + 5 * odd
            tiles = [tile(begin + i) for i in range(4)] + [tile(begin + 36 + i) for i in range(4)]
            a, b = tile(middle), tile(middle + 36)
            a, b = (turn(a), b) if odd else (a, turn(b))
            tiles.append(jnp.where(lane < 64, a, b))
            tiles += [tile(72 + begin + i) for i in range(4)]
            a = tile(72 + middle)
            tiles.append(turn(a) if odd else a)
            for i, x in enumerate(tiles):
                start = (2 * g + odd) * CHUNK + 8 * i
                terms[start : start + 8, :] = x


def finish_kernel(place, blocks, *pieces):
    lane = lanes()
    second_core = place[0] == 1
    odd = place[1] == 1
    second_half = place[2] == 1
    tiles = []
    for i in range(14):
        x = [blocks[CHUNK * q + 8 * i : CHUNK * q + 8 * i + 8, :] for q in range(8)]
        while len(x) > 1:
            x = [x[2 * j] + x[2 * j + 1] for j in range(len(x) // 2)]
        tiles.append(x[0])

    def widen(f, h):
        s = [pltpu.roll(x, 64, 1) for x in f]
        wide = [
            jnp.where(odd, jnp.where(lane < 64, a, b), c)
            for a, b, c in zip([h] + s, s + [s[3]], f + [h])
        ]
        s = [pltpu.roll(x, 96, 1) for x in wide[2:]]
        second = [jnp.where(lane < 96, s[0], s[1]), jnp.where(lane < 96, s[1], s[2]), s[2]]
        return wide[:3], second

    left = widen(tiles[0:4], tiles[8])
    right = widen(tiles[4:8], pltpu.roll(tiles[8], 64, 1))
    rest = widen(tiles[9:13], tiles[13])
    for piece, out in enumerate(pieces):
        half = second_half if piece < 2 else jnp.logical_not(second_half)
        core = second_core if piece % 2 == 0 else jnp.logical_not(second_core)
        for i in range(3):
            x = [jnp.where(core, y[1][i], y[0][i]) for y in (left, right, rest)]
            a = jnp.where(half, x[1], x[0])
            b = jnp.where(half, flip(x[2]), x[2])
            width = 128 if i < 2 else 32
            cols = slice(128 * i, 128 * i + width)
            out[0:8, cols] = a[:, :width]
            out[8:12, cols] = b[0:4, :width]


def serving_kernel(place, p00, p01, p10, p11, out):
    second_core = place[0] == 1
    second_half = place[2] == 1
    x = [[p00[...], p01[...]], [p10[...], p11[...]]]
    for member in range(2):
        swap = second_core if member == 0 else jnp.logical_not(second_core)
        near, far = (jnp.where(swap, x[i][1], x[i][0]) for i in range(2))
        h0 = jnp.where(second_half, far, near)
        h1 = jnp.where(second_half, near, far)
        for part in range(2):
            for i in range(12):
                source = h0 if i in (0, 1, 2, 3, 8, 9) else h1
                j = i % 4 + 4 * part if i < 8 else 8 + i % 2 + 2 * part
                out[member, i, part : part + 1, :] = source[j : j + 1]


def f32(*shape):
    return jax.ShapeDtypeStruct(shape, jnp.float32)


def shards(orbitals, serve_order):
    rank_fft = lax.axis_index("fft")
    rank_band = lax.axis_index("band")
    core = rank_band % 2
    line = rank_band // 2 % 8
    half = rank_band // 16
    place = jnp.stack([core, line % 2, half]).astype(jnp.int32)
    z_groups = [[y * 16 + 2 * z + c for z in range(8)] for y in range(2) for c in range(2)]
    plane_groups = [
        [(y * 16 + b) * PARTS + f for f in range(PARTS) for y in range(2)] for b in range(16)
    ]
    scale = -mixing / (NX * NY * NZ)

    coulomb = kernel_columns(rank_fft * 12, 12) * scale
    params = pltpu.CompilerParams(vmem_limit_bytes=VMEM)
    scalars = pl.BlockSpec(memory_space=pltpu.SMEM)
    whole = pl.BlockSpec(memory_space=pltpu.VMEM)

    def call(kernel, shapes, inputs, scratch=()):
        return pl.pallas_call(
            kernel,
            out_shape=shapes,
            in_specs=[scalars] + [whole] * len(inputs),
            out_specs=jax.tree.map(lambda _: whole, shapes),
            scratch_shapes=list(scratch),
            compiler_params=params,
        )(place, *inputs)

    def swap(x, bits):
        return lax.ppermute(x, "band", [(i, i ^ bits) for i in range(32)])

    def line_exchange(blocks):
        return lax.all_to_all(blocks, "band", 0, 0, axis_index_groups=z_groups, tiled=True)

    def plane_exchange(blocks):
        return lax.all_to_all(
            blocks, ("band", "fft"), 0, 0, axis_index_groups=plane_groups, tiled=True
        )

    lists = f32(LIST, 128)
    keep, send = call(halves_kernel, (lists, lists), (orbitals.reshape(2, 12, PLANE),))
    recv, coulomb = lax.optimization_barrier((swap(send, 16), coulomb))
    keep_other = swap(keep, 1)
    recv_other = swap(recv, 1)
    serving = serve_order[core]
    near = serving // 16 == half
    same = serving % 2 == core
    candidate = jnp.where(
        same, jnp.where(near, keep, recv), jnp.where(near, keep_other, recv_other)
    )
    blocks = line_exchange(candidate.reshape(8, CHUNK, 128))
    block = lax.dynamic_index_in_dim(blocks, serving // 2 % 8, 0, keepdims=True)
    served = line_exchange(jnp.broadcast_to(block, blocks.shape)).reshape(LIST, 128)

    scratch = [
        pltpu.VMEM((288, 256), jnp.float32),
        pltpu.VMEM((NY, ROWS, 256), jnp.float32),
        pltpu.VMEM((NY, ROWS, 256), jnp.float32),
    ]
    table = jnp.asarray(np.concatenate(lane_table(-1.0)))
    rows = f32(ROWS, PLANE)
    blocks, mine, other = call(
        forward_kernel,
        (f32(PARTS, 2, ROWS, BLOCK), rows, rows),
        (served, keep, recv, keep_other, recv_other, table),
        scratch,
    )
    blocks = plane_exchange(blocks.reshape(16, ROWS, BLOCK))
    tables = jnp.asarray(np.concatenate(row_tables()))
    blocks = pl.pallas_call(
        column_kernel,
        out_shape=f32(16, ROWS, BLOCK),
        in_specs=[whole] * 3,
        out_specs=whole,
        compiler_params=params,
    )(blocks, coulomb, tables)
    blocks = plane_exchange(blocks).reshape(PARTS, 2, ROWS, BLOCK)
    table = jnp.asarray(np.concatenate(lane_table(1.0)))
    short = f32(TILES, 128)
    own_near, own_far, away_near, away_far, terms = call(
        backward_kernel,
        (short, short, short, short, lists),
        (blocks, served, mine, other, table),
        scratch + [pltpu.VMEM((TILES, 128), jnp.float32)],
    )
    far = swap(own_far + swap(away_far, 1), 16)
    got = swap(away_near, 1)
    applied = call(applied_kernel, f32(12, 2, PLANE), (own_near, got, far))
    blocks = line_exchange(terms.reshape(8, CHUNK, 128)).reshape(LIST, 128)
    blocks, applied = lax.optimization_barrier((blocks, applied))
    small = f32(12, HALF)
    pieces = call(finish_kernel, (small,) * 4, (blocks,))
    pieces = [pieces[0], swap(pieces[1], 1), swap(pieces[2], 16), swap(pieces[3], 17)]
    serving_exchange = call(serving_kernel, f32(SERVE, 12, 2, HALF), pieces)
    return (applied.transpose(1, 0, 2)[None], serving_exchange.transpose(0, 2, 1, 3))


def solution(mesh):
    return jax.shard_map(
        shards,
        mesh=mesh,
        in_specs=(P("band", None, "fft", None), P()),
        out_specs=(P("band", None, "fft", None), P(None, None, "fft", "band")),
        check_vma=False,
    )
```
